256 devices in a mesh: dp: 64 (over x, y, z_lo, core), tensor: 4 (over z_hi).
Axes of the slice: x: 4, y: 4, z: 8 (z_hi: 4, z_lo: 2; z = z_hi * 2 + z_lo), core: 2. Of those that a mesh axis runs over, the one named last changes fastest.
Arguments:
- q_nope: bfloat16 [8192, 16384], P('dp', 'tensor'), may hold values from -6 to 6
- q_rope: bfloat16 [8192, 8192], P('dp', 'tensor'), may hold values from -76 to 76
- uk_weight: bfloat16 [512, 16384], P(None, 'tensor'), may hold values from -0.5 to 0.5
- uv_weight: bfloat16 [512, 16384], P(None, 'tensor'), may hold values from -1.5 to 1.5
- prompt_latent: bfloat16 [1024, 512], P('dp'), may hold values from -6 to 6
- prompt_rope: bfloat16 [1024, 64], P('dp'), may hold values from -6 to 6
- doc_latent: bfloat16 [8192, 512], P(('dp', 'tensor')), may hold values from -6 to 6
- doc_rope: bfloat16 [8192, 64], P(('dp', 'tensor')), may hold values from -6 to 6
- doc_lengths: int32 [64], P('dp'), may hold values from 32 to 128, as said below
Outputs:
- attended: bfloat16 [8192, 16384], P('dp', 'tensor')
The draws below stay inside these ranges and needn't reach their ends.
Inputs may be any that keep to these rules, and one draw needn't show every extreme that they name: `doc_lengths`: lengths lie between 32 and 128; tokens of a document at or past its length are padding.
All inputs are finite; a program needn't handle non-finite values.
Results may differ from the reference program's by a relative error of at most 0.0085.
Values may be sent and summed in bfloat16 or wider, within the bound.
A program may use at most 128 MiB of HBM per device.

```python
import jax
import jax.numpy as jnp
from jax import lax

H = 128
DN = 128
DR = 64
DV = 128
LAT = 512
DOC_LEN = 128
TOKENS = 8192
DOCS = 64
PROMPT = 1024


def draw_prompt_rope(key, part):
    key = jax.random.fold_in(key, 7)
    return jnp.clip(jax.random.normal(key, (PROMPT, DR), jnp.float32), -6.0, 6.0).astype(jnp.bfloat16)


def draw_q_rope(key, part):
    key = jax.random.fold_in(key, 11)
    return jnp.clip(jax.random.normal(key, (TOKENS, H * DR), jnp.float32), -6.0, 6.0).astype(jnp.bfloat16)


def draw_doc_lengths(key, part):
    key = jax.random.fold_in(key, 13)
    lengths = jax.random.randint(key, (DOCS,), DOC_LEN // 4, DOC_LEN + 1, dtype=jnp.int32)
    return lengths.at[0].set(DOC_LEN)


def shard_levels(rng, dims, split, smallest, largest):
    gain, own = 1.0, jax.random.fold_in(rng, 6)
    for dim, shards_of in split:
        heights = jnp.exp(jax.random.uniform(jax.random.fold_in(own, dim), (shards_of,), jnp.float32, smallest / len(split), largest / len(split)))
        gain = gain * jnp.repeat(heights, dims[dim] // shards_of).reshape([-1 if axis == dim else 1 for axis in range(len(dims))])
    return gain


def normal_values(stream_key, dims, deviation, most, split=(), held_as=jnp.bfloat16):
    values = jax.random.normal(stream_key, dims, jnp.float32) * deviation
    if len(split) > 0:
        values = shard_levels(stream_key, dims, split, -0.22, 0.18) * values
    return jnp.clip(values, min=-most, max=most).astype(held_as)


def setup_inputs(seed: int = 0) -> dict:
    keys = jax.random.split(jax.random.key(seed), 10)
    q_nope = normal_values(keys[0], (TOKENS, H * DN), 1.0, 6.0, ((0, 64), (1, 4)))
    q_rope = draw_q_rope(jax.random.fold_in(keys[9], 71), 0)
    uk_weight = normal_values(keys[2], (LAT, H * DN), DN ** -0.5, 0.5, ((1, 4),))
    uv_weight = normal_values(keys[3], (LAT, H * DV), (LAT // 32) ** -0.5, 1.5, ((1, 4),))
    prompt_latent = normal_values(keys[4], (PROMPT, LAT), 1.0, 6.0, ((0, 64),))
    prompt_rope = draw_prompt_rope(jax.random.fold_in(keys[9], 71), 0)
    doc_latent = normal_values(keys[6], (TOKENS, LAT), 1.0, 6.0, ((0, 256),))
    doc_rope = normal_values(keys[7], (TOKENS, DR), 1.0, 6.0, ((0, 256),))
    doc_lengths = draw_doc_lengths(jax.random.fold_in(keys[9], 71), 0)
    return dict(q_nope=q_nope, q_rope=q_rope, uk_weight=uk_weight, uv_weight=uv_weight, prompt_latent=prompt_latent, prompt_rope=prompt_rope, doc_latent=doc_latent, doc_rope=doc_rope, doc_lengths=doc_lengths)


def reference(q_nope, q_rope, uk_weight, uv_weight, prompt_latent, prompt_rope, doc_latent, doc_rope, doc_lengths):
    scaling = (DN + DR) ** -0.5
    up_keys = uk_weight.astype(jnp.float32).reshape(LAT, H, DN)
    up_values = uv_weight.astype(jnp.float32).reshape(LAT, H, DV)
    prompt_lat_full = prompt_latent.astype(jnp.float32)
    prompt_rope_full = prompt_rope.astype(jnp.float32)
    query_nope = q_nope.reshape(DOCS, DOC_LEN, H, DN)
    query_rope = q_rope.reshape(DOCS, DOC_LEN, H, DR)
    latent_docs = doc_latent.reshape(DOCS, DOC_LEN, LAT)
    rope_docs = doc_rope.reshape(DOCS, DOC_LEN, DR)
    position = jnp.arange(DOC_LEN)
    causal = position[:, None] >= position[None, :]
    allowed = jnp.concatenate([jnp.ones((DOC_LEN, PROMPT), dtype=bool), causal], axis=1)

    def per_document(inputs):
        nope_rows, rope_rows, latent_rows, rope_keys_doc, length = inputs
        query_lat = jnp.einsum('thd,lhd->thl', nope_rows.astype(jnp.float32), up_keys).astype(jnp.bfloat16)
        query_lat = lax.optimization_barrier(query_lat).astype(jnp.float32)
        keys_lat = jnp.concatenate([prompt_lat_full, latent_rows.astype(jnp.float32)], axis=0)
        keys_rope = jnp.concatenate([prompt_rope_full, rope_keys_doc.astype(jnp.float32)], axis=0)
        scores = (jnp.einsum('thl,kl->thk', query_lat, keys_lat)
                  + jnp.einsum('thr,kr->thk', rope_rows.astype(jnp.float32), keys_rope)) * scaling
        scores = jnp.where(allowed[:, None, :], scores, -jnp.inf)
        row_max = jnp.max(scores, axis=2, keepdims=True)
        weights = jnp.exp(scores - row_max)
        summed = jnp.sum(weights, axis=2, keepdims=True)
        rounded = lax.optimization_barrier(weights.astype(jnp.bfloat16)).astype(jnp.float32)
        out_lat = (jnp.einsum('thk,kl->thl', rounded, keys_lat) / summed).astype(jnp.bfloat16)
        out_lat = lax.optimization_barrier(out_lat).astype(jnp.float32)
        result = jnp.einsum('thl,lhv->thv', out_lat, up_values)
        is_valid = position < length
        result = jnp.where(is_valid[:, None, None], result, 0.0)
        return result.astype(jnp.bfloat16).reshape(DOC_LEN, H * DV)

    results = lax.map(per_document, (query_nope, query_rope, latent_docs, rope_docs, doc_lengths))
    return results.reshape(DOCS * DOC_LEN, H * DV)
```

```python
import functools

import jax
import jax.numpy as jnp
from jax import lax
from jax.experimental import pallas as pl
from jax.experimental.pallas import tpu as pltpu
from jax.sharding import PartitionSpec as P

MESH = pl.DeviceIdType.MESH
F32, BF16 = jnp.float32, jnp.bfloat16

DN = 128
DR = 64
DV = 128
LAT = 512
WIDE = 640
TOK = 128
HEADS = 32
GROUP = 4
N = GROUP * TOK
GROUPS = HEADS // GROUP
PROMPT = 1024
KEYS = PROMPT + TOK
SCALE = (DN + DR) ** -0.5 * 1.4426950408889634


def dot(a, b):
    return jnp.dot(a, b, preferred_element_type=F32)


def kernel(
    qn_h, qr_h, uk_h, uv_h, pl_h, pr_h, dl_h, dr_h, ln,
    out_h,
    qn, qr, uk, uv, pls, prs, dls, drs,
    keys, docs, ct, qt, s0, s1, p0, p1, mx, inv, out_v,
    lsem, osem, ssem, rsem,
):
    S, PR = (s0, s1), (p0, p1)
    me = lax.axis_index("dp")
    ten = lax.axis_index("tensor")
    x, y, zl, c = me // 16, (me // 4) % 4, (me // 2) % 2, me % 2
    a = c * x + (1 - c) * y
    b = c * y + (1 - c) * x
    g = a * 2 + zl

    def place(b_, g_):
        a_, z_ = g_ // 2, g_ % 2
        x_ = c * a_ + (1 - c) * b_
        y_ = c * b_ + (1 - c) * a_
        return (x_ * 16 + y_ * 4 + z_ * 2 + c, ten)

    near = [place(b, (g + d) % 8) for d in range(1, 8)]
    up, down = place((b + 1) % 4, g), place((b + 3) % 4, g)
    twin = (me + 1 - 2 * c, ten)
    others = [(me, (ten + d) % 4) for d in range(1, 4)]

    loads = {}

    def load(name, src, dst, k):
        loads[name] = pltpu.make_async_copy(src, dst, lsem.at[k])
        loads[name].start()

    load("pl", pl_h, pls, 0)
    load("pr", pr_h, prs, 1)
    load("dl", dl_h, dls, 2)
    load("dr", dr_h, drs, 3)
    load("qn", qn_h, qn, 4)
    load("qr", qr_h, qr, 5)
    for j in range(4):
        load("uk%d" % j, uk_h.at[:, pl.ds(j * 1024, 1024)], uk.at[:, pl.ds(j * 1024, 1024)], 6 + j)
    load("uv", uv_h, uv, 10)

    barrier = pltpu.get_barrier_semaphore()
    peers = near + [up, down, twin] + others
    for peer in peers:
        pl.semaphore_signal(barrier, inc=1, device_id=peer, device_id_type=MESH)

    for name in ("pl", "pr", "dl", "dr"):
        loads[name].wait()
    keys[c, b, g, :, :LAT] = pls[...]
    keys[c, b, g, :, LAT:] = jnp.concatenate([prs[...], jnp.zeros((16, DR), BF16)], axis=1)
    docs[ten, :, :LAT] = dls[...]
    docs[ten, :, LAT:] = jnp.concatenate([drs[...], jnp.zeros((32, DR), BF16)], axis=1)
    pl.semaphore_wait(barrier, len(peers))

    count = [0]
    sent = []

    def send(ref, peer):
        k = count[0]
        count[0] += 1
        copy = pltpu.make_async_remote_copy(
            src_ref=ref, dst_ref=ref, send_sem=ssem.at[k], recv_sem=rsem.at[k], device_id=peer, device_id_type=MESH
        )
        copy.start()
        sent.append(copy)
        return copy

    first = [send(keys.at[c, b, g], peer) for peer in near]
    doc = [send(docs.at[ten], peer) for peer in others]

    def qlat(i, _):
        zero = jnp.zeros((TOK, TOK), BF16)
        for p in range(GROUP // 2):
            cols = pl.ds(pl.multiple_of(i * N + p * 256, 256), 256)
            q = qn[:, cols]
            diag = jnp.concatenate(
                [
                    jnp.concatenate([q[:, :DN].T, zero], axis=1),
                    jnp.concatenate([zero, q[:, DN:].T], axis=1),
                ],
                axis=0,
            )
            qt[i, :LAT, p * 256 : (p + 1) * 256] = dot(uk[:, cols], diag).astype(BF16)
            r = qr[:, pl.ds(pl.multiple_of(i * (N // 2) + p * 128, 128), 128)].T
            qt[i, LAT : LAT + DR, p * 256 : (p + 1) * 256] = jnp.concatenate([r[:DR], r[DR:]], axis=1)
        qt[i, LAT + DR :, :] = jnp.zeros((WIDE - LAT - DR, N), BF16)
        return 0

    loads["qn"].wait()
    loads["qr"].wait()
    loads["uk0"].wait()
    lax.fori_loop(0, 2, qlat, 0)

    for copy in first:
        copy.wait_recv()
    lo, hi = pl.ds(0, 4), pl.ds(4, 4)
    up0 = send(keys.at[c, b, lo], up)
    down1 = send(keys.at[c, b, hi], down)
    up1 = send(keys.at[c, b, hi], up)
    down0 = send(keys.at[c, b, lo], down)
    own = send(keys.at[c, b], twin)

    loads["uk1"].wait()
    lax.fori_loop(2, 4, qlat, 0)

    prev, nxt, far = (b + 3) % 4, (b + 1) % 4, (b + 2) % 4
    up0.wait_recv()
    far0 = send(keys.at[c, prev, lo], up)
    down1.wait_recv()
    far1 = send(keys.at[c, nxt, hi], down)
    up1.wait_recv()
    t0 = send(keys.at[c, prev], twin)
    down0.wait_recv()
    t1 = send(keys.at[c, nxt], twin)

    loads["uk2"].wait()
    loads["uk3"].wait()
    lax.fori_loop(4, 8, qlat, 0)

    far0.wait_recv()
    t2 = send(keys.at[c, far, lo], twin)
    far1.wait_recv()
    t3 = send(keys.at[c, far, hi], twin)
    for copy in doc:
        copy.wait_recv()
    for copy in (own, t0, t1, t2, t3):
        copy.wait_recv()
    for copy in sent:
        copy.wait_send()

    for j in range(8):
        ct[:, j * 128 : (j + 1) * 128] = keys[j // 4, j % 4].reshape(128, WIDE)[:, :LAT].T
    ct[:, PROMPT:] = docs[...].reshape(128, WIDE)[:, :LAT].T
    loads["uv"].wait()

    key_at = lax.broadcasted_iota(jnp.int32, (TOK, TOK), 0)
    tok_at = lax.broadcasted_iota(jnp.int32, (TOK, TOK), 1)
    causal = jnp.concatenate([key_at <= tok_at] * GROUP, axis=1)
    valid = key_at < ln[0]

    def scores(i, k):
        top = None
        for j in range(0, KEYS, 256):
            if j < PROMPT:
                block = keys[j // 512, (j // 128) % 4 : (j // 128) % 4 + 2].reshape(256, WIDE)
                s = dot(block, qt[i])
            else:
                s = dot(docs[...].reshape(TOK, WIDE), qt[i])
                s = jnp.where(causal, s, -1e30)
            rows = s.shape[0]
            S[k][j : j + rows] = s
            m = jnp.max(s.reshape(rows // 8, 8, N), axis=0)
            top = m if top is None else jnp.maximum(top, m)
            yield
        mx[k] = jnp.broadcast_to(jnp.max(top, axis=0, keepdims=True) * SCALE, (8, N))
        yield

    def weights(k):
        m = mx[k][:1]
        total = jnp.zeros((8, N), F32)
        for r in range(0, KEYS, 64):
            w = jnp.exp2(S[k][r : r + 64] * SCALE - m)
            total = total + jnp.sum(w.reshape(8, 8, N), axis=0)
            PR[k][r : r + 64] = w.astype(BF16)
            yield
        inv[k] = jnp.broadcast_to(1.0 / jnp.sum(total, axis=0, keepdims=True), (8, N))
        yield

    def project(i, k):
        o = (dot(ct[...], PR[k][...]) * inv[k][:1]).astype(BF16)
        yield
        for h in range(GROUP):
            cols = pl.ds(pl.multiple_of(i * N + h * DV, DV), DV)
            v = lax.dot_general(
                o[:, h * TOK : (h + 1) * TOK], uv[:, cols], (((0,), (0,)), ((), ())), preferred_element_type=F32
            )
            out_v[:, cols] = jnp.where(valid, v, 0.0).astype(BF16)
            yield
        cols = pl.ds(pl.multiple_of(i * N, N), N)
        pltpu.make_async_copy(out_v.at[:, cols], out_h.at[:, cols], osem.at[i]).start()
        yield

    def run(*steps):
        most = max(n for _, n in steps)
        done = [0] * len(steps)
        for t in range(1, most + 1):
            for k, (step, n) in enumerate(steps):
                while done[k] * most < t * n and done[k] < n:
                    next(step, None)
                    done[k] += 1
        for step, _ in steps:
            for _ in step:
                pass

    def A(i, k):
        return scores(i, k), 6

    def B(k):
        return weights(k), 19

    def C(i, k):
        return project(i, k), GROUP + 2

    run(A(0, 0))
    run(A(1, 1), B(0))

    def body(t, _):
        i = 2 * t + 1
        run(C(i - 1, 0), A(i + 1, 0), B(1))
        run(C(i, 1), A(jnp.minimum(i + 2, GROUPS - 1), 1), B(0))
        return 0

    lax.fori_loop(0, GROUPS // 2 - 1, body, 0)
    run(C(GROUPS - 2, 0), B(1))
    run(C(GROUPS - 1, 1))
    for i in range(GROUPS):
        cols = pl.ds(i * N, N)
        pltpu.make_async_copy(out_v.at[:, cols], out_h.at[:, cols], osem.at[i]).wait()


def per_device(q_nope, q_rope, uk_weight, uv_weight, prompt_latent, prompt_rope, doc_latent, doc_rope, doc_lengths):
    hbm = pl.BlockSpec(memory_space=pl.ANY)
    copies = 20
    return pl.pallas_call(
        kernel,
        out_shape=jax.ShapeDtypeStruct((TOK, HEADS * DV), BF16),
        in_specs=[hbm] * 8 + [pl.BlockSpec(memory_space=pltpu.SMEM)],
        out_specs=hbm,
        scratch_shapes=[
            pltpu.VMEM((TOK, HEADS * DN), BF16),
            pltpu.VMEM((TOK, HEADS * DR), BF16),
            pltpu.VMEM((LAT, HEADS * DN), BF16),
            pltpu.VMEM((LAT, HEADS * DV), BF16),
            pltpu.VMEM((16, LAT), BF16),
            pltpu.VMEM((16, DR), BF16),
            pltpu.VMEM((32, LAT), BF16),
            pltpu.VMEM((32, DR), BF16),
            pltpu.VMEM((2, 4, 8, 16, WIDE), BF16),
            pltpu.VMEM((4, 32, WIDE), BF16),
            pltpu.VMEM((LAT, KEYS), BF16),
            pltpu.VMEM((GROUPS, WIDE, N), BF16),
            pltpu.VMEM((KEYS, N), F32),
            pltpu.VMEM((KEYS, N), F32),
            pltpu.VMEM((KEYS, N), BF16),
            pltpu.VMEM((KEYS, N), BF16),
            pltpu.VMEM((2, 8, N), F32),
            pltpu.VMEM((2, 8, N), F32),
            pltpu.VMEM((TOK, HEADS * DV), BF16),
            pltpu.SemaphoreType.DMA((11,)),
            pltpu.SemaphoreType.DMA((GROUPS,)),
            pltpu.SemaphoreType.DMA((24,)),
            pltpu.SemaphoreType.DMA((24,)),
        ],
        compiler_params=pltpu.CompilerParams(
            collective_id=0, has_side_effects=True, vmem_limit_bytes=56 * 2**20
        ),
        name="attend",
    )(q_nope, q_rope, uk_weight, uv_weight, prompt_latent, prompt_rope, doc_latent, doc_rope, doc_lengths)


def solution(mesh):
    return jax.shard_map(
        per_device,
        mesh=mesh,
        in_specs=(
            P("dp", "tensor"),
            P("dp", "tensor"),
            P(None, "tensor"),
            P(None, "tensor"),
            P("dp", None),
            P("dp", None),
            P(("dp", "tensor"), None),
            P(("dp", "tensor"), None),
            P("dp"),
        ),
        out_specs=P("dp", "tensor"),
        check_vma=False,
    )
```

```python
import functools

import jax
import jax.numpy as jnp
from jax import lax
from jax.experimental import pallas as pl
from jax.experimental.pallas import tpu as pltpu
from jax.sharding import PartitionSpec as P

MESH = pl.DeviceIdType.MESH
F32, BF16 = jnp.float32, jnp.bfloat16

DN = 128
DR = 64
DV = 128
LAT = 512
WIDE = 640
TOK = 128
HEADS = 32
GROUP = 4
N = GROUP * TOK
GROUPS = HEADS // GROUP
PROMPT = 1024
KEYS = PROMPT + TOK
SCALE = (DN + DR) ** -0.5 * 1.4426950408889634


def dot(a, b):
    return jnp.dot(a, b, preferred_element_type=F32)


def kernel(
    qn_h, qr_h, uk_h, uv_h, pl_h, pr_h, dl_h, dr_h, ln,
    out_h,
    qn, qr, uk, uv, pls, prs, dls, drs,
    keys, docs, ct, qt, s0, s1, p0, p1, mx, al, sm, acc, mrun, lrun, out_v,
    lsem, osem, ssem, rsem,
):
    S, PR = (s0, s1), (p0, p1)
    me = lax.axis_index("dp")
    ten = lax.axis_index("tensor")
    x, y, zl, c = me // 16, (me // 4) % 4, (me // 2) % 2, me % 2
    a = c * x + (1 - c) * y
    b = c * y + (1 - c) * x
    g = a * 2 + zl

    def place(b_, g_):
        a_, z_ = g_ // 2, g_ % 2
        x_ = c * a_ + (1 - c) * b_
        y_ = c * b_ + (1 - c) * a_
        return x_ * 16 + y_ * 4 + z_ * 2 + c

    flip = 1 - 2 * c
    near = [(place(b, (g + d) % 8), ten) for d in range(1, 8)]
    up_at, down_at = place((b + 1) % 4, g), place((b + 3) % 4, g)
    up, down = (up_at, ten), (down_at, ten)
    up_twin, down_twin = (up_at + flip, ten), (down_at + flip, ten)
    v_up = (c * ((x + 1) % 4) + (1 - c) * x) * 16 + (c * y + (1 - c) * ((y + 1) % 4)) * 4 + zl * 2 + (1 - c)
    v_down = (c * ((x + 3) % 4) + (1 - c) * x) * 16 + (c * y + (1 - c) * ((y + 3) % 4)) * 4 + zl * 2 + (1 - c)
    twin = (me + flip, ten)
    others = [(me, (ten + d) % 4) for d in range(1, 4)]

    loads = {}

    def load(name, src, dst, k):
        loads[name] = pltpu.make_async_copy(src, dst, lsem.at[k])
        loads[name].start()

    load("pl", pl_h, pls, 0)
    load("pr", pr_h, prs, 1)
    load("dl", dl_h, dls, 2)
    load("dr", dr_h, drs, 3)
    load("qn", qn_h, qn, 4)
    load("qr", qr_h, qr, 5)
    for j in range(4):
        load("uk%d" % j, uk_h.at[:, pl.ds(j * 1024, 1024)], uk.at[:, pl.ds(j * 1024, 1024)], 6 + j)
    load("uv", uv_h, uv, 10)

    barrier = pltpu.get_barrier_semaphore()
    peers = near + [up, down, up_twin, down_twin, (v_up, ten), (v_down, ten), twin] + others
    for peer in peers:
        pl.semaphore_signal(barrier, inc=1, device_id=peer, device_id_type=MESH)

    for name in ("pl", "pr", "dl", "dr"):
        loads[name].wait()
    keys[c, b, g, :, :LAT] = pls[...]
    keys[c, b, g, :, LAT:] = jnp.concatenate([prs[...], jnp.zeros((16, DR), BF16)], axis=1)
    docs[ten, :, :LAT] = dls[...]
    docs[ten, :, LAT:] = jnp.concatenate([drs[...], jnp.zeros((32, DR), BF16)], axis=1)
    pl.semaphore_wait(barrier, len(peers))

    count = [0]
    sent = []

    def send(ref, peer):
        k = count[0]
        count[0] += 1
        copy = pltpu.make_async_remote_copy(
            src_ref=ref, dst_ref=ref, send_sem=ssem.at[k], recv_sem=rsem.at[k], device_id=peer, device_id_type=MESH
        )
        copy.start()
        sent.append(copy)
        return copy

    first = [send(keys.at[c, b, g], peer) for peer in near]
    doc = [send(docs.at[ten], peer) for peer in others]

    def qlat(i, _):
        zero = jnp.zeros((TOK, TOK), BF16)
        for p in range(GROUP // 2):
            cols = pl.ds(pl.multiple_of(i * N + p * 256, 256), 256)
            q = qn[:, cols]
            diag = jnp.concatenate(
                [
                    jnp.concatenate([q[:, :DN].T, zero], axis=1),
                    jnp.concatenate([zero, q[:, DN:].T], axis=1),
                ],
                axis=0,
            )
            qt[i, :LAT, p * 256 : (p + 1) * 256] = dot(uk[:, cols], diag).astype(BF16)
            r = qr[:, pl.ds(pl.multiple_of(i * (N // 2) + p * 128, 128), 128)].T
            qt[i, LAT : LAT + DR, p * 256 : (p + 1) * 256] = jnp.concatenate([r[:DR], r[DR:]], axis=1)
        qt[i, LAT + DR :, :] = jnp.zeros((WIDE - LAT - DR, N), BF16)
        return 0

    loads["qn"].wait()
    loads["qr"].wait()
    for j in range(4):
        loads["uk%d" % j].wait()
    lax.fori_loop(0, GROUPS, qlat, 0)

    key_at = lax.broadcasted_iota(jnp.int32, (TOK, TOK), 0)
    tok_at = lax.broadcasted_iota(jnp.int32, (TOK, TOK), 1)
    causal = jnp.concatenate([key_at <= tok_at] * GROUP, axis=1)
    valid = key_at < ln[0]

    def run(*steps):
        most = max(n for _, n in steps)
        done = [0] * len(steps)
        for t in range(1, most + 1):
            for k, (step, n) in enumerate(steps):
                while done[k] * most < t * n and done[k] < n:
                    next(step, None)
                    done[k] += 1
        for step, _ in steps:
            for _ in step:
                pass

    def attend(slabs, at, start, end):
        rows = len(slabs) * TOK
        span = slice(at, at + rows)

        def slab(j):
            if slabs[j] is None:
                return docs[...].reshape(TOK, WIDE)
            return keys[slabs[j][0], slabs[j][1]].reshape(TOK, WIDE)

        for j in range(len(slabs)):
            ct[:, at + j * TOK : at + (j + 1) * TOK] = slab(j)[:, :LAT].T

        def scores(i, k):
            top = None
            for j in range(len(slabs)):
                s = dot(slab(j), qt[i])
                if slabs[j] is None:
                    s = jnp.where(causal, s, -1e30)
                S[k][j * TOK : (j + 1) * TOK] = s
                m = jnp.max(s.reshape(TOK // 8, 8, N), axis=0)
                top = m if top is None else jnp.maximum(top, m)
                yield
            new = jnp.broadcast_to(jnp.max(top, axis=0, keepdims=True) * SCALE, (8, N))
            if not start:
                old = mrun[i]
                new = jnp.maximum(old, new)
                al[k] = jnp.exp2(old - new)
            mx[k] = new
            if not end:
                mrun[i] = new
            yield

        def weights(k):
            m = mx[k][:1]
            total = jnp.zeros((8, N), F32)
            for r in range(0, rows, 64):
                w = jnp.exp2(S[k][r : r + 64] * SCALE - m)
                total = total + jnp.sum(w.reshape(8, 8, N), axis=0)
                PR[k][r : r + 64] = w.astype(BF16)
                yield
            sm[k] = total
            yield

        def project(i, k):
            total = sm[k]
            if not start:
                total = total + lrun[i] * al[k]
            if not end:
                lrun[i] = total
            inverse = 1.0 / jnp.sum(total, axis=0, keepdims=True)
            parts = []
            for r in range(0, LAT, 256):
                o = dot(ct[r : r + 256, span], PR[k][:rows])
                if not start:
                    o = o + acc[i, r : r + 256] * al[k][:1]
                if end:
                    parts.append((o * inverse).astype(BF16))
                else:
                    acc[i, r : r + 256] = o
                yield
            if not end:
                return
            o = jnp.concatenate(parts, axis=0)
            for h in range(GROUP):
                cols = pl.ds(pl.multiple_of(i * N + h * DV, DV), DV)
                v = lax.dot_general(
                    o[:, h * TOK : (h + 1) * TOK], uv[:, cols], (((0,), (0,)), ((), ())), preferred_element_type=F32
                )
                out_v[:, cols] = jnp.where(valid, v, 0.0).astype(BF16)
                yield
            cols = pl.ds(pl.multiple_of(i * N, N), N)
            pltpu.make_async_copy(out_v.at[:, cols], out_h.at[:, cols], osem.at[i]).start()
            yield

        def A(i, k):
            return scores(i, k), len(slabs) + 1

        def B(k):
            return weights(k), rows // 64 + 1

        def C(i, k):
            return project(i, k), 2 + (GROUP + 1 if end else 0)

        run(A(0, 0))
        run(A(1, 1), B(0))

        def body(t, _):
            i = 2 * t + 1
            run(C(i - 1, 0), A(i + 1, 0), B(1))
            run(C(i, 1), A(i + 2, 1), B(0))
            return 0

        lax.fori_loop(0, GROUPS // 2 - 1, body, 0)
        run(C(GROUPS - 2, 0), B(1))
        run(C(GROUPS - 1, 1))

    for copy in first:
        copy.wait_recv()
    lo, hi = pl.ds(0, 4), pl.ds(4, 4)
    up0 = send(keys.at[c, b, lo], up)
    down1 = send(keys.at[c, b, hi], down)
    own = send(keys.at[c, b], twin)
    up1 = send(keys.at[c, b, hi], up)
    down0 = send(keys.at[c, b, lo], down)
    own.wait_recv()
    d = 1 - c
    attend([(c, b), (d, a)], 0, True, False)

    prev, nxt, far = (b + 3) % 4, (b + 1) % 4, (b + 2) % 4
    up0.wait_recv()
    far0 = send(keys.at[c, prev, lo], up)
    far2 = send(keys.at[c, prev, lo], up_twin)
    down1.wait_recv()
    far1 = send(keys.at[c, nxt, hi], down)
    far3 = send(keys.at[c, nxt, hi], down_twin)
    up1.wait_recv()
    t0 = send(keys.at[c, prev], twin)
    down0.wait_recv()
    t1 = send(keys.at[c, nxt], twin)
    for copy in doc:
        copy.wait_recv()
    attend([None, (c, prev), (c, nxt)], 256, False, False)

    for copy in (far0, far1, far2, far3, t0, t1):
        copy.wait_recv()
    loads["uv"].wait()
    attend([(d, (a + 3) % 4), (d, (a + 1) % 4), (c, far), (d, (a + 2) % 4)], 640, False, True)
    for copy in sent:
        copy.wait_send()
    for i in range(GROUPS):
        cols = pl.ds(i * N, N)
        pltpu.make_async_copy(out_v.at[:, cols], out_h.at[:, cols], osem.at[i]).wait()


def per_device(q_nope, q_rope, uk_weight, uv_weight, prompt_latent, prompt_rope, doc_latent, doc_rope, doc_lengths):
    hbm = pl.BlockSpec(memory_space=pl.ANY)
    return pl.pallas_call(
        kernel,
        out_shape=jax.ShapeDtypeStruct((TOK, HEADS * DV), BF16),
        in_specs=[hbm] * 8 + [pl.BlockSpec(memory_space=pltpu.SMEM)],
        out_specs=hbm,
        scratch_shapes=[
            pltpu.VMEM((TOK, HEADS * DN), BF16),
            pltpu.VMEM((TOK, HEADS * DR), BF16),
            pltpu.VMEM((LAT, HEADS * DN), BF16),
            pltpu.VMEM((LAT, HEADS * DV), BF16),
            pltpu.VMEM((16, LAT), BF16),
            pltpu.VMEM((16, DR), BF16),
            pltpu.VMEM((32, LAT), BF16),
            pltpu.VMEM((32, DR), BF16),
            pltpu.VMEM((2, 4, 8, 16, WIDE), BF16),
            pltpu.VMEM((4, 32, WIDE), BF16),
            pltpu.VMEM((LAT, KEYS), BF16),
            pltpu.VMEM((GROUPS, WIDE, N), BF16),
            pltpu.VMEM((512, N), F32),
            pltpu.VMEM((512, N), F32),
            pltpu.VMEM((512, N), BF16),
            pltpu.VMEM((512, N), BF16),
            pltpu.VMEM((2, 8, N), F32),
            pltpu.VMEM((2, 8, N), F32),
            pltpu.VMEM((2, 8, N), F32),
            pltpu.VMEM((GROUPS, LAT, N), F32),
            pltpu.VMEM((GROUPS, 8, N), F32),
            pltpu.VMEM((GROUPS, 8, N), F32),
            pltpu.VMEM((TOK, HEADS * DV), BF16),
            pltpu.SemaphoreType.DMA((11,)),
            pltpu.SemaphoreType.DMA((GROUPS,)),
            pltpu.SemaphoreType.DMA((24,)),
            pltpu.SemaphoreType.DMA((24,)),
        ],
        compiler_params=pltpu.CompilerParams(
            collective_id=0, has_side_effects=True, vmem_limit_bytes=56 * 2**20
        ),
        name="attend",
    )(q_nope, q_rope, uk_weight, uv_weight, prompt_latent, prompt_rope, doc_latent, doc_rope, doc_lengths)


def solution(mesh):
    return jax.shard_map(
        per_device,
        mesh=mesh,
        in_specs=(
            P("dp", "tensor"),
            P("dp", "tensor"),
            P(None, "tensor"),
            P(None, "tensor"),
            P("dp", None),
            P("dp", None),
            P(("dp", "tensor"), None),
            P(("dp", "tensor"), None),
            P("dp"),
        ),
        out_specs=P("dp", "tensor"),
        check_vma=False,
    )
```

```python
import functools

import jax
import jax.numpy as jnp
from jax import lax
from jax.experimental import pallas as pl
from jax.experimental.pallas import tpu as pltpu
from jax.sharding import PartitionSpec as P

MESH = pl.DeviceIdType.MESH
F32, BF16 = jnp.float32, jnp.bfloat16

DN = 128
DR = 64
DV = 128
LAT = 512
WIDE = 640
TOK = 128
HEADS = 32
GROUP = 4
N = GROUP * TOK
GROUPS = HEADS // GROUP
PROMPT = 1024
KEYS = PROMPT + TOK
SCALE = (DN + DR) ** -0.5 * 1.4426950408889634


def dot(a, b):
    return jnp.dot(a, b, preferred_element_type=F32)


def kernel(
    qn_h, qr_h, uk_h, uv_h, pl_h, pr_h, dl_h, dr_h, ln,
    out_h,
    qn, qr, uk, uv, pls, prs, dls, drs,
    keys, docs, ct, qt, s0, s1, p0, p1, mx, al, sm, acc, mrun, lrun, out_v,
    lsem, osem, ssem, rsem,
):
    S, PR = (s0, s1), (p0, p1)
    me = lax.axis_index("dp")
    ten = lax.axis_index("tensor")
    x, y, zl, c = me // 16, (me // 4) % 4, (me // 2) % 2, me % 2
    a = c * x + (1 - c) * y
    b = c * y + (1 - c) * x
    g = a * 2 + zl

    def place(b_, g_):
        a_, z_ = g_ // 2, g_ % 2
        x_ = c * a_ + (1 - c) * b_
        y_ = c * b_ + (1 - c) * a_
        return x_ * 16 + y_ * 4 + z_ * 2 + c

    flip = 1 - 2 * c
    near = [(place(b, (g + d) % 8), ten) for d in range(1, 8)]
    up, down = (place((b + 1) % 4, g), ten), (place((b + 3) % 4, g), ten)
    far_at = place((b + 2) % 4, g)
    far, far_twin = (far_at, ten), (far_at + flip, ten)
    v_x = c * ((x + 2) % 4) + (1 - c) * x
    v_y = c * y + (1 - c) * ((y + 2) % 4)
    v_far = (v_x * 16 + v_y * 4 + zl * 2 + 1 - c, ten)
    twin = (me + flip, ten)
    t_up, t_down = (me, (ten + 1) % 4), (me, (ten + 3) % 4)

    loads = {}

    def load(name, src, dst, k):
        loads[name] = pltpu.make_async_copy(src, dst, lsem.at[k])
        loads[name].start()

    load("pl", pl_h, pls, 0)
    load("pr", pr_h, prs, 1)
    load("dl", dl_h, dls, 2)
    load("dr", dr_h, drs, 3)
    load("qn", qn_h, qn, 4)
    load("qr", qr_h, qr, 5)
    for j in range(4):
        load("uk%d" % j, uk_h.at[:, pl.ds(j * 1024, 1024)], uk.at[:, pl.ds(j * 1024, 1024)], 6 + j)
    load("uv", uv_h, uv, 10)

    barrier = pltpu.get_barrier_semaphore()
    peers = near + [up, down, far, far_twin, v_far, twin, t_up, t_down]
    for peer in peers:
        pl.semaphore_signal(barrier, inc=1, device_id=peer, device_id_type=MESH)

    for name in ("pl", "pr", "dl", "dr"):
        loads[name].wait()
    keys[c, b, g, :, :LAT] = pls[...]
    keys[c, b, g, :, LAT:] = jnp.concatenate([prs[...], jnp.zeros((16, DR), BF16)], axis=1)
    docs[ten, :, :LAT] = dls[...]
    docs[ten, :, LAT:] = jnp.concatenate([drs[...], jnp.zeros((32, DR), BF16)], axis=1)
    pl.semaphore_wait(barrier, len(peers))

    count = [0]
    sent = []

    def send(ref, peer):
        k = count[0]
        count[0] += 1
        copy = pltpu.make_async_remote_copy(
            src_ref=ref, dst_ref=ref, send_sem=ssem.at[k], recv_sem=rsem.at[k], device_id=peer, device_id_type=MESH
        )
        copy.start()
        sent.append(copy)
        return copy

    first = [send(keys.at[c, b, g], peer) for peer in near]
    doc_up, doc_down = send(docs.at[ten], t_up), send(docs.at[ten], t_down)

    def qlat(i, _):
        zero = jnp.zeros((TOK, TOK), BF16)
        for p in range(GROUP // 2):
            cols = pl.ds(pl.multiple_of(i * N + p * 256, 256), 256)
            q = qn[:, cols]
            diag = jnp.concatenate(
                [
                    jnp.concatenate([q[:, :DN].T, zero], axis=1),
                    jnp.concatenate([zero, q[:, DN:].T], axis=1),
                ],
                axis=0,
            )
            qt[i, :LAT, p * 256 : (p + 1) * 256] = dot(uk[:, cols], diag).astype(BF16)
            r = qr[:, pl.ds(pl.multiple_of(i * (N // 2) + p * 128, 128), 128)].T
            qt[i, LAT : LAT + DR, p * 256 : (p + 1) * 256] = jnp.concatenate([r[:DR], r[DR:]], axis=1)
        qt[i, LAT + DR :, :] = jnp.zeros((WIDE - LAT - DR, N), BF16)
        return 0

    loads["qn"].wait()
    loads["qr"].wait()
    for j in range(4):
        loads["uk%d" % j].wait()
        lax.fori_loop(2 * j, 2 * j + 2, qlat, 0)

    key_at = lax.broadcasted_iota(jnp.int32, (TOK, TOK), 0)
    tok_at = lax.broadcasted_iota(jnp.int32, (TOK, TOK), 1)
    causal = jnp.concatenate([key_at <= tok_at] * GROUP, axis=1)
    valid = key_at < ln[0]

    def run(*steps):
        most = max(n for _, n in steps)
        done = [0] * len(steps)
        for t in range(1, most + 1):
            for k, (step, n) in enumerate(steps):
                while done[k] * most < t * n and done[k] < n:
                    next(step, None)
                    done[k] += 1
        for step, _ in steps:
            for _ in step:
                pass

    def attend(slabs, at, start, end):
        rows = len(slabs) * TOK
        span = slice(at, at + rows)

        def slab(j):
            if slabs[j] is None:
                return docs[...].reshape(TOK, WIDE)
            return keys[slabs[j][0], slabs[j][1]].reshape(TOK, WIDE)

        for j in range(len(slabs)):
            ct[:, at + j * TOK : at + (j + 1) * TOK] = slab(j)[:, :LAT].T

        def scores(i, k):
            top = None
            step = 4
            for j in range(0, len(slabs), step):
                some = slabs[j : j + step]
                s = dot(jnp.concatenate([slab(j + n) for n in range(len(some))], axis=0), qt[i])
                for n, which in enumerate(some):
                    part = s[n * TOK : (n + 1) * TOK]
                    if which is None:
                        part = jnp.where(causal, part, -1e30)
                    S[k][(j + n) * TOK : (j + n + 1) * TOK] = part
                    m = jnp.max(part.reshape(TOK // 8, 8, N), axis=0)
                    top = m if top is None else jnp.maximum(top, m)
                yield
            new = jnp.broadcast_to(jnp.max(top, axis=0, keepdims=True) * SCALE, (8, N))
            if not start:
                old = mrun[i]
                new = jnp.maximum(old, new)
                al[k] = jnp.exp2(old - new)
            mx[k] = new
            if not end:
                mrun[i] = new
            yield

        def weights(k):
            m = mx[k][:1]
            total = jnp.zeros((8, N), F32)
            for r in range(0, rows, 64):
                w = jnp.exp2(S[k][r : r + 64] * SCALE - m)
                total = total + jnp.sum(w.reshape(8, 8, N), axis=0)
                PR[k][r : r + 64] = w.astype(BF16)
                yield
            sm[k] = total
            yield

        def project(i, k):
            total = sm[k]
            if not start:
                fade = al[k]
                total = total + lrun[i] * fade
            if not end:
                lrun[i] = total
            inverse = 1.0 / jnp.sum(total, axis=0, keepdims=True)
            parts = []
            for r in range(0, LAT, 512):
                o = dot(ct[r : r + 512, span], PR[k][:rows])
                if not start:
                    o = o + acc[i, r : r + 512] * fade[:1]
                if end:
                    parts.append((o * inverse).astype(BF16))
                else:
                    acc[i, r : r + 512] = o
                yield
            if not end:
                return
            o = jnp.concatenate(parts, axis=0)
            for h in range(GROUP):
                cols = pl.ds(pl.multiple_of(i * N + h * DV, DV), DV)
                v = lax.dot_general(
                    o[:, h * TOK : (h + 1) * TOK], uv[:, cols], (((0,), (0,)), ((), ())), preferred_element_type=F32
                )
                out_v[:, cols] = jnp.where(valid, v, 0.0).astype(BF16)
                yield
            cols = pl.ds(pl.multiple_of(i * N, N), N)
            pltpu.make_async_copy(out_v.at[:, cols], out_h.at[:, cols], osem.at[i]).start()
            yield

        def A(i, k):
            return scores(i, k), -(-len(slabs) // 4) + 1

        def B(k):
            return weights(k), rows // 64 + 1

        def C(i, k):
            return project(i, k), 1 + (GROUP + 1 if end else 0)

        return A, B, C

    def loop(stages):
        A, B, C = stages

        def body(t, _):
            i = 2 * t + 1
            run(A(i + 1, 0), B(1), C(i - 1, 0))
            run(A(i + 2, 1), B(0), C(i, 1))
            return 0

        lax.fori_loop(0, GROUPS // 2 - 1, body, 0)

    def join(old, new):
        run(new[0](0, 0), old[1](1), old[2](GROUPS - 2, 0))
        run(new[0](1, 1), new[1](0), old[2](GROUPS - 1, 1))

    for copy in first:
        copy.wait_recv()
    own = send(keys.at[c, b], twin)
    up0, down0 = send(keys.at[c, b], up), send(keys.at[c, b], down)
    prev, nxt, opp, d = (b + 3) % 4, (b + 1) % 4, (b + 2) % 4, 1 - c
    doc_up.wait_recv()
    doc_far0 = send(docs.at[(ten + 3) % 4, pl.ds(0, 16)], t_up)
    doc_down.wait_recv()
    doc_far1 = send(docs.at[(ten + 1) % 4, pl.ds(16, 16)], t_down)
    own.wait_recv()
    one = attend([(c, b), (d, a)], 0, True, False)
    run(one[0](0, 0))
    run(one[0](1, 1), one[1](0))
    loop(one)

    up0.wait_recv()
    down0.wait_recv()
    t0, t1 = send(keys.at[c, prev], twin), send(keys.at[c, nxt], twin)
    far0, far1 = send(keys.at[c, b], far), send(keys.at[c, b], far_twin)
    doc_far0.wait_recv()
    doc_far1.wait_recv()
    two = attend([None, (c, prev), (c, nxt)], 256, False, False)
    join(one, two)
    loop(two)

    for copy in (far0, far1, t0, t1):
        copy.wait_recv()
    loads["uv"].wait()
    three = attend([(d, (a + 3) % 4), (d, (a + 1) % 4), (c, opp), (d, (a + 2) % 4)], 640, False, True)
    join(two, three)
    loop(three)
    run(three[2](GROUPS - 2, 0), three[1](1))
    run(three[2](GROUPS - 1, 1))
    for copy in sent:
        copy.wait_send()
    for i in range(GROUPS):
        cols = pl.ds(i * N, N)
        pltpu.make_async_copy(out_v.at[:, cols], out_h.at[:, cols], osem.at[i]).wait()


def per_device(q_nope, q_rope, uk_weight, uv_weight, prompt_latent, prompt_rope, doc_latent, doc_rope, doc_lengths):
    hbm = pl.BlockSpec(memory_space=pl.ANY)
    return pl.pallas_call(
        kernel,
        out_shape=jax.ShapeDtypeStruct((TOK, HEADS * DV), BF16),
        in_specs=[hbm] * 8 + [pl.BlockSpec(memory_space=pltpu.SMEM)],
        out_specs=hbm,
        scratch_shapes=[
            pltpu.VMEM((TOK, HEADS * DN), BF16),
            pltpu.VMEM((TOK, HEADS * DR), BF16),
            pltpu.VMEM((LAT, HEADS * DN), BF16),
            pltpu.VMEM((LAT, HEADS * DV), BF16),
            pltpu.VMEM((16, LAT), BF16),
            pltpu.VMEM((16, DR), BF16),
            pltpu.VMEM((32, LAT), BF16),
            pltpu.VMEM((32, DR), BF16),
            pltpu.VMEM((2, 4, 8, 16, WIDE), BF16),
            pltpu.VMEM((4, 32, WIDE), BF16),
            pltpu.VMEM((LAT, KEYS), BF16),
            pltpu.VMEM((GROUPS, WIDE, N), BF16),
            pltpu.VMEM((512, N), F32),
            pltpu.VMEM((512, N), F32),
            pltpu.VMEM((512, N), BF16),
            pltpu.VMEM((512, N), BF16),
            pltpu.VMEM((2, 8, N), F32),
            pltpu.VMEM((2, 8, N), F32),
            pltpu.VMEM((2, 8, N), F32),
            pltpu.VMEM((GROUPS, LAT, N), F32),
            pltpu.VMEM((GROUPS, 8, N), F32),
            pltpu.VMEM((GROUPS, 8, N), F32),
            pltpu.VMEM((TOK, HEADS * DV), BF16),
            pltpu.SemaphoreType.DMA((11,)),
            pltpu.SemaphoreType.DMA((GROUPS,)),
            pltpu.SemaphoreType.DMA((24,)),
            pltpu.SemaphoreType.DMA((24,)),
        ],
        compiler_params=pltpu.CompilerParams(
            collective_id=0, has_side_effects=True, vmem_limit_bytes=56 * 2**20
        ),
        name="attend",
    )(q_nope, q_rope, uk_weight, uv_weight, prompt_latent, prompt_rope, doc_latent, doc_rope, doc_lengths)


def solution(mesh):
    return jax.shard_map(
        per_device,
        mesh=mesh,
        in_specs=(
            P("dp", "tensor"),
            P("dp", "tensor"),
            P(None, "tensor"),
            P(None, "tensor"),
            P("dp", None),
            P("dp", None),
            P(("dp", "tensor"), None),
            P(("dp", "tensor"), None),
            P("dp"),
        ),
        out_specs=P("dp", "tensor"),
        check_vma=False,
    )
```

```python
import functools

import jax
import jax.numpy as jnp
from jax import lax
from jax.experimental import pallas as pl
from jax.experimental.pallas import tpu as pltpu
from jax.sharding import PartitionSpec as P

MESH = pl.DeviceIdType.MESH
F32, BF16 = jnp.float32, jnp.bfloat16

DN = 128
DR = 64
DV = 128
LAT = 512
WIDE = 640
TOK = 128
HEADS = 32
GROUP = 4
N = GROUP * TOK
GROUPS = HEADS // GROUP
PROMPT = 1024
KEYS = PROMPT + TOK
SCALE = (DN + DR) ** -0.5 * 1.4426950408889634


def dot(a, b):
    return jnp.dot(a, b, preferred_element_type=F32)


def kernel(
    qn_h, qr_h, uk_h, uv_h, pl_h, pr_h, dl_h, dr_h, ln,
    out_h,
    qn, qr, uk, uv, pls, prs, dls, drs,
    keys, docs, ct, qt, s0, s1, p0, p1, mx, al, sm, acc, mrun, lrun, out_v,
    lsem, osem, ssem, rsem,
):
    S, PR = (s0, s1), (p0, p1)
    me = lax.axis_index("dp")
    ten = lax.axis_index("tensor")
    x, y, zl, c = me // 16, (me // 4) % 4, (me // 2) % 2, me % 2
    a = c * x + (1 - c) * y
    b = c * y + (1 - c) * x
    g = a * 2 + zl

    def place(b_, g_):
        a_, z_ = g_ // 2, g_ % 2
        x_ = c * a_ + (1 - c) * b_
        y_ = c * b_ + (1 - c) * a_
        return x_ * 16 + y_ * 4 + z_ * 2 + c

    flip = 1 - 2 * c
    near = []
    for d in range(1, 8):
        at = (g + d) % 8
        cross = (at + zl) % 2 * ((at // 2 + a) % 2)
        near.append((place(b, at), (ten + cross * (3 - 2 * zl)) % 4))
    up, down = (place((b + 1) % 4, g), ten), (place((b + 3) % 4, g), ten)
    far_at = place((b + 2) % 4, g)
    far, far_twin = (far_at, ten), (far_at + flip, ten)
    v_x = c * ((x + 2) % 4) + (1 - c) * x
    v_y = c * y + (1 - c) * ((y + 2) % 4)
    v_far = (v_x * 16 + v_y * 4 + zl * 2 + 1 - c, ten)
    twin = (me + flip, ten)
    t_up, t_down = (me, (ten + 1) % 4), (me, (ten + 3) % 4)

    loads = {}

    def load(name, src, dst, k):
        loads[name] = pltpu.make_async_copy(src, dst, lsem.at[k])
        loads[name].start()

    load("pl", pl_h, pls, 0)
    load("pr", pr_h, prs, 1)
    load("dl", dl_h, dls, 2)
    load("dr", dr_h, drs, 3)
    load("qn", qn_h, qn, 4)
    load("qr", qr_h, qr, 5)
    for j in range(4):
        load("uk%d" % j, uk_h.at[:, pl.ds(j * 1024, 1024)], uk.at[:, pl.ds(j * 1024, 1024)], 6 + j)
    load("uv", uv_h, uv, 10)

    barrier = pltpu.get_barrier_semaphore()
    peers = near + [up, down, far, far_twin, v_far, twin, t_up, t_down]
    for peer in peers:
        pl.semaphore_signal(barrier, inc=1, device_id=peer, device_id_type=MESH)

    for name in ("pl", "pr", "dl", "dr"):
        loads[name].wait()
    keys[c, b, g, :, :LAT] = pls[...]
    keys[c, b, g, :, LAT:] = jnp.concatenate([prs[...], jnp.zeros((16, DR), BF16)], axis=1)
    docs[ten, :, :LAT] = dls[...]
    docs[ten, :, LAT:] = jnp.concatenate([drs[...], jnp.zeros((32, DR), BF16)], axis=1)
    pl.semaphore_wait(barrier, len(peers))

    count = [0]
    sent = []

    def cross_copy(ref, peer):
        k = count[0]
        count[0] += 1
        copy = pltpu.make_async_remote_copy(
            src_ref=ref, dst_ref=ref, send_sem=ssem.at[k], recv_sem=rsem.at[k], device_id=peer, device_id_type=MESH
        )
        sent.append(copy)
        return copy

    def send(ref, peer):
        copy = cross_copy(ref, peer)
        copy.start()
        return copy

    first = [send(keys.at[c, b, g], peer) for peer in near]

    def qlat(i, _):
        zero = jnp.zeros((TOK, TOK), BF16)
        for p in range(GROUP // 2):
            cols = pl.ds(pl.multiple_of(i * N + p * 256, 256), 256)
            q = qn[:, cols]
            diag = jnp.concatenate(
                [
                    jnp.concatenate([q[:, :DN].T, zero], axis=1),
                    jnp.concatenate([zero, q[:, DN:].T], axis=1),
                ],
                axis=0,
            )
            qt[i, :LAT, p * 256 : (p + 1) * 256] = (dot(uk[:, cols], diag) * SCALE).astype(BF16)
            r = qr[:, pl.ds(pl.multiple_of(i * (N // 2) + p * 128, 128), 128)].T
            qt[i, LAT : LAT + DR, p * 256 : (p + 1) * 256] = (jnp.concatenate([r[:DR], r[DR:]], axis=1).astype(F32) * SCALE).astype(BF16)
        qt[i, LAT + DR :, :] = jnp.zeros((WIDE - LAT - DR, N), BF16)
        return 0

    loads["qn"].wait()
    loads["qr"].wait()
    for j in range(4):
        loads["uk%d" % j].wait()
        lax.fori_loop(2 * j, 2 * j + 2, qlat, 0)

    key_at = lax.broadcasted_iota(jnp.int32, (TOK, TOK), 0)
    tok_at = lax.broadcasted_iota(jnp.int32, (TOK, TOK), 1)
    causal = jnp.concatenate([key_at <= tok_at] * GROUP, axis=1)
    valid = key_at < ln[0]

    def run(*steps):
        most = max(n for _, n in steps)
        done = [0] * len(steps)
        for t in range(1, most + 1):
            for k, (step, n) in enumerate(steps):
                while done[k] * most < t * n and done[k] < n:
                    next(step, None)
                    done[k] += 1
        for step, _ in steps:
            for _ in step:
                pass

    def attend(slabs, at, start, end):
        rows = len(slabs) * TOK
        span = slice(at, at + rows)

        def slab(j):
            if slabs[j] is None:
                return docs[...].reshape(TOK, WIDE)
            return keys[slabs[j][0], slabs[j][1]].reshape(TOK, WIDE)

        for j in range(len(slabs)):
            ct[:, at + j * TOK : at + (j + 1) * TOK] = slab(j)[:, :LAT].T

        def scores(i, k):
            top = None
            step = 5
            for j in range(0, len(slabs), step):
                some = slabs[j : j + step]
                s = dot(jnp.concatenate([slab(j + n) for n in range(len(some))], axis=0), qt[i])
                for n, which in enumerate(some):
                    part = s[n * TOK : (n + 1) * TOK]
                    if which is None:
                        part = jnp.where(causal, part, -1e30)
                    S[k][(j + n) * TOK : (j + n + 1) * TOK] = part
                    m = jnp.max(part.reshape(TOK // 8, 8, N), axis=0)
                    top = m if top is None else jnp.maximum(top, m)
                yield
            new = jnp.broadcast_to(jnp.max(top, axis=0, keepdims=True), (8, N))
            if not start:
                old = mrun[i]
                new = jnp.maximum(old, new)
                al[k] = jnp.exp2(old - new)
            mx[k] = new
            if not end:
                mrun[i] = new
            yield

        def weights(k):
            m = mx[k][:1]
            total = jnp.zeros((8, N), F32)
            for r in range(0, rows, 64):
                w = jnp.exp2(S[k][r : r + 64] - m)
                total = total + jnp.sum(w.reshape(8, 8, N), axis=0)
                PR[k][r : r + 64] = w.astype(BF16)
                yield
            sm[k] = total
            yield

        def project(i, k):
            total = sm[k]
            if not start:
                fade = al[k]
                total = total + lrun[i] * fade
            if not end:
                lrun[i] = total
            inverse = 1.0 / jnp.sum(total, axis=0, keepdims=True)
            parts = []
            for r in range(0, LAT, 512):
                o = dot(ct[r : r + 512, span], PR[k][:rows])
                if not start:
                    o = o + acc[i, r : r + 512] * fade[:1]
                if end:
                    parts.append((o * inverse).astype(BF16))
                else:
                    acc[i, r : r + 512] = o
                yield
            if not end:
                return
            o = jnp.concatenate(parts, axis=0)
            for h in range(GROUP):
                cols = pl.ds(pl.multiple_of(i * N + h * DV, DV), DV)
                v = lax.dot_general(
                    o[:, h * TOK : (h + 1) * TOK], uv[:, cols], (((0,), (0,)), ((), ())), preferred_element_type=F32
                )
                out_v[:, cols] = jnp.where(valid, v, 0.0).astype(BF16)
                yield
            cols = pl.ds(pl.multiple_of(i * N, N), N)
            pltpu.make_async_copy(out_v.at[:, cols], out_h.at[:, cols], osem.at[i]).start()
            yield

        def A(i, k):
            return scores(i, k), -(-len(slabs) // 5) + 1

        def B(k):
            return weights(k), rows // 64 + 1

        def C(i, k):
            return project(i, k), 1 + (GROUP + 1 if end else 0)

        return A, B, C

    def loop(stages, extra=None):
        A, B, C = stages

        def body(t, _):
            i = 2 * t + 1
            if extra is not None:
                pl.when(t == 1)(extra)
            run(A(i + 1, 0), B(1), C(i - 1, 0))
            run(A(i + 2, 1), B(0), C(i, 1))
            return 0

        lax.fori_loop(0, GROUPS // 2 - 1, body, 0)

    def join(old, new):
        run(new[0](0, 0), old[1](1), old[2](GROUPS - 2, 0))
        run(new[0](1, 1), new[1](0), old[2](GROUPS - 1, 1))

    for copy in first:
        copy.wait_recv()
    own = send(keys.at[c, b], twin)
    up0, down0 = send(keys.at[c, b], up), send(keys.at[c, b], down)
    prev, nxt, opp, d = (b + 3) % 4, (b + 1) % 4, (b + 2) % 4, 1 - c
    doc_up, doc_down = send(docs.at[ten], t_up), send(docs.at[ten], t_down)
    own.wait_recv()
    crossing = [cross_copy(keys.at[c, b], peer) for peer in (far, far_twin)]

    def cross_over():
        for copy in (up0, down0):
            copy.wait_send()
        sent[:] = [copy for copy in sent if copy is not up0 and copy is not down0]
        for copy in crossing:
            copy.start()

    one = attend([(c, b), (d, a)], 0, True, False)
    run(one[0](0, 0))
    run(one[0](1, 1), one[1](0))
    loop(one, cross_over)
    far0, far1 = crossing
    doc_up.wait_recv()
    doc_far0 = send(docs.at[(ten + 3) % 4, pl.ds(0, 16)], t_up)
    doc_down.wait_recv()
    doc_far1 = send(docs.at[(ten + 1) % 4, pl.ds(16, 16)], t_down)

    up0.wait_recv()
    down0.wait_recv()
    t0, t1 = send(keys.at[c, prev], twin), send(keys.at[c, nxt], twin)
    two = attend([(c, prev), (c, nxt)], 256, False, False)
    join(one, two)
    loop(two)

    for copy in (doc_far0, doc_far1, far0, far1, t0, t1):
        copy.wait_recv()
    loads["uv"].wait()
    three = attend([None, (d, (a + 3) % 4), (d, (a + 1) % 4), (c, opp), (d, (a + 2) % 4)], 512, False, True)
    join(two, three)
    loop(three)
    run(three[2](GROUPS - 2, 0), three[1](1))
    run(three[2](GROUPS - 1, 1))
    for copy in sent:
        copy.wait_send()
    for i in range(GROUPS):
        cols = pl.ds(i * N, N)
        pltpu.make_async_copy(out_v.at[:, cols], out_h.at[:, cols], osem.at[i]).wait()


def per_device(q_nope, q_rope, uk_weight, uv_weight, prompt_latent, prompt_rope, doc_latent, doc_rope, doc_lengths):
    hbm = pl.BlockSpec(memory_space=pl.ANY)
    return pl.pallas_call(
        kernel,
        out_shape=jax.ShapeDtypeStruct((TOK, HEADS * DV), BF16),
        in_specs=[hbm] * 8 + [pl.BlockSpec(memory_space=pltpu.SMEM)],
        out_specs=hbm,
        scratch_shapes=[
            pltpu.VMEM((TOK, HEADS * DN), BF16),
            pltpu.VMEM((TOK, HEADS * DR), BF16),
            pltpu.VMEM((LAT, HEADS * DN), BF16),
            pltpu.VMEM((LAT, HEADS * DV), BF16),
            pltpu.VMEM((16, LAT), BF16),
            pltpu.VMEM((16, DR), BF16),
            pltpu.VMEM((32, LAT), BF16),
            pltpu.VMEM((32, DR), BF16),
            pltpu.VMEM((2, 4, 8, 16, WIDE), BF16),
            pltpu.VMEM((4, 32, WIDE), BF16),
            pltpu.VMEM((LAT, KEYS), BF16),
            pltpu.VMEM((GROUPS, WIDE, N), BF16),
            pltpu.VMEM((640, N), F32),
            pltpu.VMEM((640, N), F32),
            pltpu.VMEM((640, N), BF16),
            pltpu.VMEM((640, N), BF16),
            pltpu.VMEM((2, 8, N), F32),
            pltpu.VMEM((2, 8, N), F32),
            pltpu.VMEM((2, 8, N), F32),
            pltpu.VMEM((GROUPS, LAT, N), F32),
            pltpu.VMEM((GROUPS, 8, N), F32),
            pltpu.VMEM((GROUPS, 8, N), F32),
            pltpu.VMEM((TOK, HEADS * DV), BF16),
            pltpu.SemaphoreType.DMA((11,)),
            pltpu.SemaphoreType.DMA((GROUPS,)),
            pltpu.SemaphoreType.DMA((24,)),
            pltpu.SemaphoreType.DMA((24,)),
        ],
        compiler_params=pltpu.CompilerParams(
            collective_id=0, has_side_effects=True, vmem_limit_bytes=56 * 2**20
        ),
        name="attend",
    )(q_nope, q_rope, uk_weight, uv_weight, prompt_latent, prompt_rope, doc_latent, doc_rope, doc_lengths)


def solution(mesh):
    return jax.shard_map(
        per_device,
        mesh=mesh,
        in_specs=(
            P("dp", "tensor"),
            P("dp", "tensor"),
            P(None, "tensor"),
            P(None, "tensor"),
            P("dp", None),
            P("dp", None),
            P(("dp", "tensor"), None),
            P(("dp", "tensor"), None),
            P("dp"),
        ),
        out_specs=P("dp", "tensor"),
        check_vma=False,
    )
```

```python
import functools

import jax
import jax.numpy as jnp
from jax import lax
from jax.experimental import pallas as pl
from jax.experimental.pallas import tpu as pltpu
from jax.sharding import PartitionSpec as P

MESH = pl.DeviceIdType.MESH
F32, BF16 = jnp.float32, jnp.bfloat16

DN = 128
DR = 64
DV = 128
LAT = 512
WIDE = 640
TOK = 128
HEADS = 32
GROUP = 8
N = GROUP * TOK
GROUPS = HEADS // GROUP
PROMPT = 1024
KEYS = PROMPT + TOK
SCALE = (DN + DR) ** -0.5 * 1.4426950408889634


def dot(a, b):
    return jnp.dot(a, b, preferred_element_type=F32)


def kernel(
    qn_h, qr_h, uk_h, uv_h, pl_h, pr_h, dl_h, dr_h, ln,
    out_h,
    qn, qr, uk, uv, pls, prs, dls, drs,
    keys, docs, ct, qt, s0, s1, p0, p1, mx, al, sm, acc, mrun, lrun, out_v,
    lsem, osem, ssem, rsem,
):
    S, PR = (s0, s1), (p0, p1)
    me = lax.axis_index("dp")
    ten = lax.axis_index("tensor")
    x, y, zl, c = me // 16, (me // 4) % 4, (me // 2) % 2, me % 2
    a = c * x + (1 - c) * y
    b = c * y + (1 - c) * x
    g = a * 2 + zl

    def place(b_, g_):
        a_, z_ = g_ // 2, g_ % 2
        x_ = c * a_ + (1 - c) * b_
        y_ = c * b_ + (1 - c) * a_
        return x_ * 16 + y_ * 4 + z_ * 2 + c

    flip = 1 - 2 * c
    near = []
    for d in range(1, 8):
        at = (g + d) % 8
        cross = (at + zl) % 2 * ((at // 2 + a) % 2)
        near.append((place(b, at), (ten + cross * (3 - 2 * zl)) % 4))
    up, down = (place((b + 1) % 4, g), ten), (place((b + 3) % 4, g), ten)
    far_at = place((b + 2) % 4, g)
    far, far_twin = (far_at, ten), (far_at + flip, ten)
    v_x = c * ((x + 2) % 4) + (1 - c) * x
    v_y = c * y + (1 - c) * ((y + 2) % 4)
    v_far = (v_x * 16 + v_y * 4 + zl * 2 + 1 - c, ten)
    twin = (me + flip, ten)
    t_up, t_down = (me, (ten + 1) % 4), (me, (ten + 3) % 4)

    loads = {}

    def load(name, src, dst, k):
        loads[name] = pltpu.make_async_copy(src, dst, lsem.at[k])
        loads[name].start()

    load("pl", pl_h, pls, 0)
    load("pr", pr_h, prs, 1)
    load("dl", dl_h, dls, 2)
    load("dr", dr_h, drs, 3)
    load("qn", qn_h, qn, 4)
    load("qr", qr_h, qr, 5)
    for j in range(4):
        load("uk%d" % j, uk_h.at[:, pl.ds(j * 1024, 1024)], uk.at[:, pl.ds(j * 1024, 1024)], 6 + j)
    load("uv", uv_h, uv, 10)

    barrier = pltpu.get_barrier_semaphore()
    peers = near + [up, down, far, far_twin, v_far, twin, t_up, t_down]
    for peer in peers:
        pl.semaphore_signal(barrier, inc=1, device_id=peer, device_id_type=MESH)

    for name in ("pl", "pr", "dl", "dr"):
        loads[name].wait()
    keys[c, b, g, :, :LAT] = pls[...]
    keys[c, b, g, :, LAT:] = jnp.concatenate([prs[...], jnp.zeros((16, DR), BF16)], axis=1)
    docs[ten, :, :LAT] = dls[...]
    docs[ten, :, LAT:] = jnp.concatenate([drs[...], jnp.zeros((32, DR), BF16)], axis=1)
    pl.semaphore_wait(barrier, len(peers))

    count = [0]
    sent = []

    def cross_copy(ref, peer):
        k = count[0]
        count[0] += 1
        copy = pltpu.make_async_remote_copy(
            src_ref=ref, dst_ref=ref, send_sem=ssem.at[k], recv_sem=rsem.at[k], device_id=peer, device_id_type=MESH
        )
        sent.append(copy)
        return copy

    def send(ref, peer):
        copy = cross_copy(ref, peer)
        copy.start()
        return copy

    first = [send(keys.at[c, b, g], peer) for peer in near]

    def qlat(i, _):
        zero = jnp.zeros((TOK, TOK), BF16)
        for p in range(GROUP // 2):
            cols = pl.ds(pl.multiple_of(i * N + p * 256, 256), 256)
            q = qn[:, cols]
            diag = jnp.concatenate(
                [
                    jnp.concatenate([q[:, :DN].T, zero], axis=1),
                    jnp.concatenate([zero, q[:, DN:].T], axis=1),
                ],
                axis=0,
            )
            qt[i, :LAT, p * 256 : (p + 1) * 256] = dot(uk[:, cols], diag).astype(BF16)
            r = qr[:, pl.ds(pl.multiple_of(i * (N // 2) + p * 128, 128), 128)].T
            qt[i, LAT : LAT + DR, p * 256 : (p + 1) * 256] = jnp.concatenate([r[:DR], r[DR:]], axis=1)
        qt[i, LAT + DR :, :] = jnp.zeros((WIDE - LAT - DR, N), BF16)
        return 0

    loads["qn"].wait()
    loads["qr"].wait()
    for j in range(4):
        loads["uk%d" % j].wait()
        lax.fori_loop(GROUPS * j // 4, GROUPS * (j + 1) // 4, qlat, 0)

    key_at = lax.broadcasted_iota(jnp.int32, (TOK, TOK), 0)
    tok_at = lax.broadcasted_iota(jnp.int32, (TOK, TOK), 1)
    causal = jnp.concatenate([key_at <= tok_at] * GROUP, axis=1)
    valid = key_at < ln[0]

    def run(*steps):
        most = max(n for _, n in steps)
        done = [0] * len(steps)
        for t in range(1, most + 1):
            for k, (step, n) in enumerate(steps):
                while done[k] * most < t * n and done[k] < n:
                    next(step, None)
                    done[k] += 1
        for step, _ in steps:
            for _ in step:
                pass

    def attend(slabs, at, start, end):
        rows = len(slabs) * TOK
        span = slice(at, at + rows)

        def slab(j):
            if slabs[j] is None:
                return docs[...].reshape(TOK, WIDE)
            return keys[slabs[j][0], slabs[j][1]].reshape(TOK, WIDE)

        for j in range(len(slabs)):
            ct[:, at + j * TOK : at + (j + 1) * TOK] = slab(j)[:, :LAT].T

        def scores(i, k):
            top = None
            step = 5
            for j in range(0, len(slabs), step):
                some = slabs[j : j + step]
                s = dot(jnp.concatenate([slab(j + n) for n in range(len(some))], axis=0), qt[i])
                for n, which in enumerate(some):
                    part = s[n * TOK : (n + 1) * TOK]
                    if which is None:
                        part = jnp.where(causal, part, -1e30)
                    S[k][(j + n) * TOK : (j + n + 1) * TOK] = part
                    m = jnp.max(part.reshape(TOK // 8, 8, N), axis=0)
                    top = m if top is None else jnp.maximum(top, m)
                yield
            new = jnp.broadcast_to(jnp.max(top, axis=0, keepdims=True) * SCALE, (8, N))
            if not start:
                old = mrun[i]
                new = jnp.maximum(old, new)
                al[k] = jnp.exp2(old - new)
            mx[k] = new
            if not end:
                mrun[i] = new
            yield

        def weights(k):
            m = mx[k][:1]
            total = jnp.zeros((8, N), F32)
            for r in range(0, rows, 64):
                w = jnp.exp2(S[k][r : r + 64] * SCALE - m)
                total = total + jnp.sum(w.reshape(8, 8, N), axis=0)
                PR[k][r : r + 64] = w.astype(BF16)
                yield
            sm[k] = total
            yield

        def project(i, k):
            total = sm[k]
            if not start:
                fade = al[k]
                total = total + lrun[i] * fade
            if not end:
                lrun[i] = total
            inverse = 1.0 / jnp.sum(total, axis=0, keepdims=True)
            parts = []
            for r in range(0, LAT, 512):
                o = dot(ct[r : r + 512, span], PR[k][:rows])
                if not start:
                    o = o + acc[i, r : r + 512] * fade[:1]
                if end:
                    parts.append((o * inverse).astype(BF16))
                else:
                    acc[i, r : r + 512] = o
                yield
            if not end:
                return
            o = jnp.concatenate(parts, axis=0)
            for h in range(GROUP):
                cols = pl.ds(pl.multiple_of(i * N + h * DV, DV), DV)
                v = lax.dot_general(
                    o[:, h * TOK : (h + 1) * TOK], uv[:, cols], (((0,), (0,)), ((), ())), preferred_element_type=F32
                )
                out_v[:, cols] = jnp.where(valid, v, 0.0).astype(BF16)
                yield
            cols = pl.ds(pl.multiple_of(i * N, N), N)
            pltpu.make_async_copy(out_v.at[:, cols], out_h.at[:, cols], osem.at[i]).start()
            yield

        def A(i, k):
            return scores(i, k), -(-len(slabs) // 5) + 1

        def B(k):
            return weights(k), rows // 64 + 1

        def C(i, k):
            return project(i, k), 1 + (GROUP + 1 if end else 0)

        return A, B, C

    def loop(stages, extra=None):
        A, B, C = stages

        def body(t, _):
            i = 2 * t + 1
            if extra is not None:
                pl.when(t == 0)(extra)
            run(A(i + 1, 0), B(1), C(i - 1, 0))
            run(A(i + 2, 1), B(0), C(i, 1))
            return 0

        lax.fori_loop(0, GROUPS // 2 - 1, body, 0)

    def join(old, new):
        run(new[0](0, 0), old[1](1), old[2](GROUPS - 2, 0))
        run(new[0](1, 1), new[1](0), old[2](GROUPS - 1, 1))

    for copy in first:
        copy.wait_recv()
    own = send(keys.at[c, b], twin)
    up0, down0 = send(keys.at[c, b], up), send(keys.at[c, b], down)
    prev, nxt, opp, d = (b + 3) % 4, (b + 1) % 4, (b + 2) % 4, 1 - c
    doc_up, doc_down = send(docs.at[ten], t_up), send(docs.at[ten], t_down)
    own.wait_recv()
    crossing = [cross_copy(keys.at[c, b], peer) for peer in (far, far_twin)]

    def cross_over():
        for copy in (up0, down0):
            copy.wait_send()
        sent[:] = [copy for copy in sent if copy is not up0 and copy is not down0]
        for copy in crossing:
            copy.start()

    one = attend([(c, b), (d, a)], 0, True, False)
    run(one[0](0, 0))
    run(one[0](1, 1), one[1](0))
    loop(one, cross_over)
    far0, far1 = crossing
    doc_up.wait_recv()
    doc_far0 = send(docs.at[(ten + 3) % 4, pl.ds(0, 16)], t_up)
    doc_down.wait_recv()
    doc_far1 = send(docs.at[(ten + 1) % 4, pl.ds(16, 16)], t_down)

    up0.wait_recv()
    down0.wait_recv()
    t0, t1 = send(keys.at[c, prev], twin), send(keys.at[c, nxt], twin)
    two = attend([(c, prev), (c, nxt)], 256, False, False)
    join(one, two)
    loop(two)

    for copy in (doc_far0, doc_far1, far0, far1, t0, t1):
        copy.wait_recv()
    loads["uv"].wait()
    three = attend([None, (d, (a + 3) % 4), (d, (a + 1) % 4), (c, opp), (d, (a + 2) % 4)], 512, False, True)
    join(two, three)
    loop(three)
    run(three[2](GROUPS - 2, 0), three[1](1))
    run(three[2](GROUPS - 1, 1))
    for copy in sent:
        copy.wait_send()
    for i in range(GROUPS):
        cols = pl.ds(i * N, N)
        pltpu.make_async_copy(out_v.at[:, cols], out_h.at[:, cols], osem.at[i]).wait()


def per_device(q_nope, q_rope, uk_weight, uv_weight, prompt_latent, prompt_rope, doc_latent, doc_rope, doc_lengths):
    hbm = pl.BlockSpec(memory_space=pl.ANY)
    return pl.pallas_call(
        kernel,
        out_shape=jax.ShapeDtypeStruct((TOK, HEADS * DV), BF16),
        in_specs=[hbm] * 8 + [pl.BlockSpec(memory_space=pltpu.SMEM)],
        out_specs=hbm,
        scratch_shapes=[
            pltpu.VMEM((TOK, HEADS * DN), BF16),
            pltpu.VMEM((TOK, HEADS * DR), BF16),
            pltpu.VMEM((LAT, HEADS * DN), BF16),
            pltpu.VMEM((LAT, HEADS * DV), BF16),
            pltpu.VMEM((16, LAT), BF16),
            pltpu.VMEM((16, DR), BF16),
            pltpu.VMEM((32, LAT), BF16),
            pltpu.VMEM((32, DR), BF16),
            pltpu.VMEM((2, 4, 8, 16, WIDE), BF16),
            pltpu.VMEM((4, 32, WIDE), BF16),
            pltpu.VMEM((LAT, KEYS), BF16),
            pltpu.VMEM((GROUPS, WIDE, N), BF16),
            pltpu.VMEM((640, N), F32),
            pltpu.VMEM((640, N), F32),
            pltpu.VMEM((640, N), BF16),
            pltpu.VMEM((640, N), BF16),
            pltpu.VMEM((2, 8, N), F32),
            pltpu.VMEM((2, 8, N), F32),
            pltpu.VMEM((2, 8, N), F32),
            pltpu.VMEM((GROUPS, LAT, N), F32),
            pltpu.VMEM((GROUPS, 8, N), F32),
            pltpu.VMEM((GROUPS, 8, N), F32),
            pltpu.VMEM((TOK, HEADS * DV), BF16),
            pltpu.SemaphoreType.DMA((11,)),
            pltpu.SemaphoreType.DMA((GROUPS,)),
            pltpu.SemaphoreType.DMA((24,)),
            pltpu.SemaphoreType.DMA((24,)),
        ],
        compiler_params=pltpu.CompilerParams(
            collective_id=0, has_side_effects=True, vmem_limit_bytes=56 * 2**20
        ),
        name="attend",
    )(q_nope, q_rope, uk_weight, uv_weight, prompt_latent, prompt_rope, doc_latent, doc_rope, doc_lengths)


def solution(mesh):
    return jax.shard_map(
        per_device,
        mesh=mesh,
        in_specs=(
            P("dp", "tensor"),
            P("dp", "tensor"),
            P(None, "tensor"),
            P(None, "tensor"),
            P("dp", None),
            P("dp", None),
            P(("dp", "tensor"), None),
            P(("dp", "tensor"), None),
            P("dp"),
        ),
        out_specs=P("dp", "tensor"),
        check_vma=False,
    )
```

```python
import functools

import jax
import jax.numpy as jnp
from jax import lax
from jax.experimental import pallas as pl
from jax.experimental.pallas import tpu as pltpu
from jax.sharding import PartitionSpec as P

MESH = pl.DeviceIdType.MESH
F32, BF16 = jnp.float32, jnp.bfloat16

DN = 128
DR = 64
DV = 128
LAT = 512
WIDE = 640
TOK = 128
HEADS = 32
GROUP = 8
N = GROUP * TOK
GROUPS = HEADS // GROUP
PROMPT = 1024
KEYS = PROMPT + TOK
SCALE = (DN + DR) ** -0.5 * 1.4426950408889634


def dot(a, b):
    return jnp.dot(a, b, preferred_element_type=F32)


def kernel(
    qn_h, qr_h, uk_h, uv_h, pl_h, pr_h, dl_h, dr_h, ln,
    out_h,
    qn, qr, uk, uv, pls, prs, dls, drs,
    keys, docs, ct, qt, s0, s1, p0, p1, mx, al, sm, acc, mrun, lrun, out_v,
    lsem, osem, ssem, rsem,
):
    S, PR = (s0, s1), (p0, p1)
    me = lax.axis_index("dp")
    ten = lax.axis_index("tensor")
    x, y, zl, c = me // 16, (me // 4) % 4, (me // 2) % 2, me % 2
    a = c * x + (1 - c) * y
    b = c * y + (1 - c) * x
    g = a * 2 + zl

    def place(b_, g_):
        a_, z_ = g_ // 2, g_ % 2
        x_ = c * a_ + (1 - c) * b_
        y_ = c * b_ + (1 - c) * a_
        return x_ * 16 + y_ * 4 + z_ * 2 + c

    flip = 1 - 2 * c
    near = []
    for d in range(1, 8):
        at = (g + d) % 8
        cross = (at + zl) % 2 * ((at // 2 + a) % 2)
        near.append((place(b, at), (ten + cross * (3 - 2 * zl)) % 4))
    up, down = (place((b + 1) % 4, g), ten), (place((b + 3) % 4, g), ten)
    far_at = place((b + 2) % 4, g)
    far, far_twin = (far_at, ten), (far_at + flip, ten)
    v_x = c * ((x + 2) % 4) + (1 - c) * x
    v_y = c * y + (1 - c) * ((y + 2) % 4)
    v_far = (v_x * 16 + v_y * 4 + zl * 2 + 1 - c, ten)
    twin = (me + flip, ten)
    t_up, t_down = (me, (ten + 1) % 4), (me, (ten + 3) % 4)

    loads = {}

    def load(name, src, dst, k):
        loads[name] = pltpu.make_async_copy(src, dst, lsem.at[k])
        loads[name].start()

    load("pl", pl_h, pls, 0)
    load("pr", pr_h, prs, 1)
    load("dl", dl_h, dls, 2)
    load("dr", dr_h, drs, 3)
    load("qn", qn_h, qn, 4)
    load("qr", qr_h, qr, 5)
    for j in range(4):
        load("uk%d" % j, uk_h.at[:, pl.ds(j * 1024, 1024)], uk.at[:, pl.ds(j * 1024, 1024)], 6 + j)
    load("uv", uv_h, uv, 10)

    barrier = pltpu.get_barrier_semaphore()
    peers = near + [up, down, far, far_twin, v_far, twin, t_up, t_down]
    for peer in peers:
        pl.semaphore_signal(barrier, inc=1, device_id=peer, device_id_type=MESH)

    for name in ("pl", "pr", "dl", "dr"):
        loads[name].wait()
    keys[c, b, g, :, :LAT] = pls[...]
    keys[c, b, g, :, LAT:] = jnp.concatenate([prs[...], jnp.zeros((16, DR), BF16)], axis=1)
    docs[ten, :, :LAT] = dls[...]
    docs[ten, :, LAT:] = jnp.concatenate([drs[...], jnp.zeros((32, DR), BF16)], axis=1)
    pl.semaphore_wait(barrier, len(peers))

    count = [0]
    sent = []

    def cross_copy(ref, peer):
        k = count[0]
        count[0] += 1
        copy = pltpu.make_async_remote_copy(
            src_ref=ref, dst_ref=ref, send_sem=ssem.at[k], recv_sem=rsem.at[k], device_id=peer, device_id_type=MESH
        )
        sent.append(copy)
        return copy

    def send(ref, peer):
        copy = cross_copy(ref, peer)
        copy.start()
        return copy

    first = [send(keys.at[c, b, g], peer) for peer in near]

    def qlat(i, _):
        zero = jnp.zeros((TOK, TOK), BF16)
        for p in range(GROUP // 2):
            cols = pl.ds(pl.multiple_of(i * N + p * 256, 256), 256)
            q = qn[:, cols]
            diag = jnp.concatenate(
                [
                    jnp.concatenate([q[:, :DN].T, zero], axis=1),
                    jnp.concatenate([zero, q[:, DN:].T], axis=1),
                ],
                axis=0,
            )
            qt[i, :LAT, p * 256 : (p + 1) * 256] = dot(uk[:, cols], diag).astype(BF16)
            r = qr[:, pl.ds(pl.multiple_of(i * (N // 2) + p * 128, 128), 128)].T
            qt[i, LAT : LAT + DR, p * 256 : (p + 1) * 256] = jnp.concatenate([r[:DR], r[DR:]], axis=1)
        qt[i, LAT + DR :, :] = jnp.zeros((WIDE - LAT - DR, N), BF16)
        return 0

    loads["qn"].wait()
    loads["qr"].wait()
    for j in range(4):
        loads["uk%d" % j].wait()
        lax.fori_loop(GROUPS * j // 4, GROUPS * (j + 1) // 4, qlat, 0)

    key_at = lax.broadcasted_iota(jnp.int32, (TOK, TOK), 0)
    tok_at = lax.broadcasted_iota(jnp.int32, (TOK, TOK), 1)
    causal = jnp.concatenate([key_at <= tok_at] * GROUP, axis=1)
    valid = key_at < ln[0]

    def run(*steps):
        most = max(n for _, n in steps)
        done = [0] * len(steps)
        for t in range(1, most + 1):
            for k, (step, n) in enumerate(steps):
                while done[k] * most < t * n and done[k] < n:
                    next(step, None)
                    done[k] += 1
        for step, _ in steps:
            for _ in step:
                pass

    def attend(slabs, at, start, end):
        rows = len(slabs) * TOK
        span = slice(at, at + rows)

        def slab(j):
            if slabs[j] is None:
                return docs[...].reshape(TOK, WIDE)
            return keys[slabs[j][0], slabs[j][1]].reshape(TOK, WIDE)

        for j in range(len(slabs)):
            ct[:, at + j * TOK : at + (j + 1) * TOK] = slab(j)[:, :LAT].T

        def scores(i, k):
            top = None
            step = 5
            for j in range(0, len(slabs), step):
                some = slabs[j : j + step]
                s = dot(jnp.concatenate([slab(j + n) for n in range(len(some))], axis=0), qt[i])
                for n, which in enumerate(some):
                    part = s[n * TOK : (n + 1) * TOK]
                    if which is None:
                        part = jnp.where(causal, part, -1e30)
                    S[k][(j + n) * TOK : (j + n + 1) * TOK] = part
                    m = jnp.max(part.reshape(TOK // 8, 8, N), axis=0)
                    top = m if top is None else jnp.maximum(top, m)
                yield
            new = jnp.broadcast_to(jnp.max(top, axis=0, keepdims=True) * SCALE, (8, N))
            if not start:
                old = mrun[i]
                new = jnp.maximum(old, new)
                al[k] = jnp.exp2(old - new)
            mx[k] = new
            if not end:
                mrun[i] = new
            yield

        def weights(k):
            m = mx[k][:1]
            total = jnp.zeros((8, N), F32)
            for r in range(0, rows, 64):
                w = jnp.exp2(S[k][r : r + 64] * SCALE - m)
                total = total + jnp.sum(w.reshape(8, 8, N), axis=0)
                PR[k][r : r + 64] = w.astype(BF16)
                yield
            sm[k] = total
            yield

        def project(i, k):
            total = sm[k]
            if not start:
                fade = al[k]
                total = total + lrun[i] * fade
            if not end:
                lrun[i] = total
            inverse = 1.0 / jnp.sum(total, axis=0, keepdims=True)
            parts = []
            for r in range(0, LAT, 256):
                o = dot(ct[r : r + 256, span], PR[k][:rows])
                if not start:
                    o = o + acc[i, r : r + 256] * fade[:1]
                if end:
                    parts.append((o * inverse).astype(BF16))
                else:
                    acc[i, r : r + 256] = o
                yield
            if not end:
                return
            o = jnp.concatenate(parts, axis=0)
            for h in range(GROUP):
                cols = pl.ds(pl.multiple_of(i * N + h * DV, DV), DV)
                v = lax.dot_general(
                    o[:, h * TOK : (h + 1) * TOK], uv[:, cols], (((0,), (0,)), ((), ())), preferred_element_type=F32
                )
                out_v[:, cols] = jnp.where(valid, v, 0.0).astype(BF16)
                yield
            cols = pl.ds(pl.multiple_of(i * N, N), N)
            pltpu.make_async_copy(out_v.at[:, cols], out_h.at[:, cols], osem.at[i]).start()
            yield

        def A(i, k):
            return scores(i, k), -(-len(slabs) // 5) + 1

        def B(k):
            return weights(k), rows // 64 + 1

        def C(i, k):
            return project(i, k), 2 + (GROUP + 1 if end else 0)

        return A, B, C

    def loop(stages, extra=None):
        A, B, C = stages

        def body(t, _):
            i = 2 * t + 1
            if extra is not None:
                pl.when(t == 0)(extra)
            run(A(i + 1, 0), B(1), C(i - 1, 0))
            run(A(i + 2, 1), B(0), C(i, 1))
            return 0

        lax.fori_loop(0, GROUPS // 2 - 1, body, 0)

    def join(old, new):
        run(new[0](0, 0), old[1](1), old[2](GROUPS - 2, 0))
        run(new[0](1, 1), new[1](0), old[2](GROUPS - 1, 1))

    for copy in first:
        copy.wait_recv()
    own = send(keys.at[c, b], twin)
    up0, down0 = send(keys.at[c, b], up), send(keys.at[c, b], down)
    prev, nxt, opp, d = (b + 3) % 4, (b + 1) % 4, (b + 2) % 4, 1 - c
    doc_up, doc_down = send(docs.at[ten], t_up), send(docs.at[ten], t_down)
    own.wait_recv()
    crossing = [cross_copy(keys.at[c, b], peer) for peer in (far, far_twin)]

    def cross_over():
        for copy in (up0, down0):
            copy.wait_send()
        sent[:] = [copy for copy in sent if copy is not up0 and copy is not down0]
        for copy in crossing:
            copy.start()

    one = attend([(c, b), (d, a)], 0, True, False)
    run(one[0](0, 0))
    run(one[0](1, 1), one[1](0))
    loop(one, cross_over)
    far0, far1 = crossing
    doc_up.wait_recv()
    doc_far0 = send(docs.at[(ten + 3) % 4, pl.ds(0, 16)], t_up)
    doc_down.wait_recv()
    doc_far1 = send(docs.at[(ten + 1) % 4, pl.ds(16, 16)], t_down)

    up0.wait_recv()
    down0.wait_recv()
    t0, t1 = send(keys.at[c, prev], twin), send(keys.at[c, nxt], twin)
    two = attend([(c, prev), (c, nxt)], 256, False, False)
    join(one, two)
    loop(two)

    for copy in (doc_far0, doc_far1, t0, t1):
        copy.wait_recv()
    three = attend([None, (d, (a + 3) % 4), (d, (a + 1) % 4)], 512, False, False)
    join(two, three)
    loop(three)

    for copy in (far0, far1):
        copy.wait_recv()
    loads["uv"].wait()
    four = attend([(c, opp), (d, (a + 2) % 4)], 896, False, True)
    join(three, four)
    loop(four)
    run(four[2](GROUPS - 2, 0), four[1](1))
    run(four[2](GROUPS - 1, 1))
    for copy in sent:
        copy.wait_send()
    for i in range(GROUPS):
        cols = pl.ds(i * N, N)
        pltpu.make_async_copy(out_v.at[:, cols], out_h.at[:, cols], osem.at[i]).wait()


def per_device(q_nope, q_rope, uk_weight, uv_weight, prompt_latent, prompt_rope, doc_latent, doc_rope, doc_lengths):
    hbm = pl.BlockSpec(memory_space=pl.ANY)
    return pl.pallas_call(
        kernel,
        out_shape=jax.ShapeDtypeStruct((TOK, HEADS * DV), BF16),
        in_specs=[hbm] * 8 + [pl.BlockSpec(memory_space=pltpu.SMEM)],
        out_specs=hbm,
        scratch_shapes=[
            pltpu.VMEM((TOK, HEADS * DN), BF16),
            pltpu.VMEM((TOK, HEADS * DR), BF16),
            pltpu.VMEM((LAT, HEADS * DN), BF16),
            pltpu.VMEM((LAT, HEADS * DV), BF16),
            pltpu.VMEM((16, LAT), BF16),
            pltpu.VMEM((16, DR), BF16),
            pltpu.VMEM((32, LAT), BF16),
            pltpu.VMEM((32, DR), BF16),
            pltpu.VMEM((2, 4, 8, 16, WIDE), BF16),
            pltpu.VMEM((4, 32, WIDE), BF16),
            pltpu.VMEM((LAT, KEYS), BF16),
            pltpu.VMEM((GROUPS, WIDE, N), BF16),
            pltpu.VMEM((384, N), F32),
            pltpu.VMEM((384, N), F32),
            pltpu.VMEM((384, N), BF16),
            pltpu.VMEM((384, N), BF16),
            pltpu.VMEM((2, 8, N), F32),
            pltpu.VMEM((2, 8, N), F32),
            pltpu.VMEM((2, 8, N), F32),
            pltpu.VMEM((GROUPS, LAT, N), F32),
            pltpu.VMEM((GROUPS, 8, N), F32),
            pltpu.VMEM((GROUPS, 8, N), F32),
            pltpu.VMEM((TOK, HEADS * DV), BF16),
            pltpu.SemaphoreType.DMA((11,)),
            pltpu.SemaphoreType.DMA((GROUPS,)),
            pltpu.SemaphoreType.DMA((24,)),
            pltpu.SemaphoreType.DMA((24,)),
        ],
        compiler_params=pltpu.CompilerParams(
            collective_id=0, has_side_effects=True, vmem_limit_bytes=56 * 2**20
        ),
        name="attend",
    )(q_nope, q_rope, uk_weight, uv_weight, prompt_latent, prompt_rope, doc_latent, doc_rope, doc_lengths)


def solution(mesh):
    return jax.shard_map(
        per_device,
        mesh=mesh,
        in_specs=(
            P("dp", "tensor"),
            P("dp", "tensor"),
            P(None, "tensor"),
            P(None, "tensor"),
            P("dp", None),
            P("dp", None),
            P(("dp", "tensor"), None),
            P(("dp", "tensor"), None),
            P("dp"),
        ),
        out_specs=P("dp", "tensor"),
        check_vma=False,
    )
```

```python
import functools

import jax
import jax.numpy as jnp
from jax import lax
from jax.experimental import pallas as pl
from jax.experimental.pallas import tpu as pltpu
from jax.sharding import PartitionSpec as P

MESH = pl.DeviceIdType.MESH
F32, BF16 = jnp.float32, jnp.bfloat16

DN = 128
DR = 64
DV = 128
LAT = 512
WIDE = 640
TOK = 128
HEADS = 32
GROUP = 8
N = GROUP * TOK
GROUPS = HEADS // GROUP
PROMPT = 1024
KEYS = PROMPT + TOK
SCALE = (DN + DR) ** -0.5 * 1.4426950408889634


def dot(a, b):
    return jnp.dot(a, b, preferred_element_type=F32)


def kernel(
    qn_h, qr_h, uk_h, uv_h, pl_h, pr_h, dl_h, dr_h, ln,
    out_h,
    qn, qr, uk, uv, pls, prs, dls, drs,
    keys, docs, ct, qt, s0, s1, p0, p1, mx, al, sm, acc, mrun, lrun, out_v,
    lsem, osem, ssem, rsem,
):
    S, PR = (s0, s1), (p0, p1)
    me = lax.axis_index("dp")
    ten = lax.axis_index("tensor")
    x, y, zl, c = me // 16, (me // 4) % 4, (me // 2) % 2, me % 2
    a = c * x + (1 - c) * y
    b = c * y + (1 - c) * x
    g = a * 2 + zl

    def place(b_, g_):
        a_, z_ = g_ // 2, g_ % 2
        x_ = c * a_ + (1 - c) * b_
        y_ = c * b_ + (1 - c) * a_
        return x_ * 16 + y_ * 4 + z_ * 2 + c

    flip = 1 - 2 * c
    near = [(place(b, (g + d) % 8), ten) for d in range(1, 8)]
    up, down = (place((b + 1) % 4, g), ten), (place((b + 3) % 4, g), ten)
    far_at = place((b + 2) % 4, g)
    far, far_twin = (far_at, ten), (far_at + flip, ten)
    v_x = c * ((x + 2) % 4) + (1 - c) * x
    v_y = c * y + (1 - c) * ((y + 2) % 4)
    v_far = (v_x * 16 + v_y * 4 + zl * 2 + 1 - c, ten)
    twin = (me + flip, ten)
    t_up, t_down = (me, (ten + 1) % 4), (me, (ten + 3) % 4)

    loads = {}

    def load(name, src, dst, k):
        loads[name] = pltpu.make_async_copy(src, dst, lsem.at[k])
        loads[name].start()

    load("pl", pl_h, pls, 0)
    load("pr", pr_h, prs, 1)
    load("dl", dl_h, dls, 2)
    load("dr", dr_h, drs, 3)
    load("qn", qn_h, qn, 4)
    load("qr", qr_h, qr, 5)
    for j in range(4):
        load("uk%d" % j, uk_h.at[:, pl.ds(j * 1024, 1024)], uk.at[:, pl.ds(j * 1024, 1024)], 6 + j)
    load("uv", uv_h, uv, 10)

    barrier = pltpu.get_barrier_semaphore()
    peers = near + [up, down, far, far_twin, v_far, twin, t_up, t_down]
    for peer in peers:
        pl.semaphore_signal(barrier, inc=1, device_id=peer, device_id_type=MESH)

    for name in ("pl", "pr", "dl", "dr"):
        loads[name].wait()
    keys[c, b, g, :, :LAT] = pls[...]
    keys[c, b, g, :, LAT:] = jnp.concatenate([prs[...], jnp.zeros((16, DR), BF16)], axis=1)
    docs[ten, :, :LAT] = dls[...]
    docs[ten, :, LAT:] = jnp.concatenate([drs[...], jnp.zeros((32, DR), BF16)], axis=1)
    pl.semaphore_wait(barrier, len(peers))

    count = [0]
    sent = []

    def cross_copy(ref, peer):
        k = count[0]
        count[0] += 1
        copy = pltpu.make_async_remote_copy(
            src_ref=ref, dst_ref=ref, send_sem=ssem.at[k], recv_sem=rsem.at[k], device_id=peer, device_id_type=MESH
        )
        sent.append(copy)
        return copy

    def send(ref, peer):
        copy = cross_copy(ref, peer)
        copy.start()
        return copy

    first = [send(keys.at[c, b, g], peer) for peer in near]

    def qlat(i, _):
        zero = jnp.zeros((TOK, TOK), BF16)
        for p in range(GROUP // 2):
            cols = pl.ds(pl.multiple_of(i * N + p * 256, 256), 256)
            q = qn[:, cols]
            diag = jnp.concatenate(
                [
                    jnp.concatenate([q[:, :DN].T, zero], axis=1),
                    jnp.concatenate([zero, q[:, DN:].T], axis=1),
                ],
                axis=0,
            )
            qt[i, :LAT, p * 256 : (p + 1) * 256] = dot(uk[:, cols], diag).astype(BF16)
            r = qr[:, pl.ds(pl.multiple_of(i * (N // 2) + p * 128, 128), 128)].T
            qt[i, LAT : LAT + DR, p * 256 : (p + 1) * 256] = jnp.concatenate([r[:DR], r[DR:]], axis=1)
        qt[i, LAT + DR :, :] = jnp.zeros((WIDE - LAT - DR, N), BF16)
        return 0

    loads["qn"].wait()
    loads["qr"].wait()
    for j in range(4):
        loads["uk%d" % j].wait()
        lax.fori_loop(GROUPS * j // 4, GROUPS * (j + 1) // 4, qlat, 0)

    key_at = lax.broadcasted_iota(jnp.int32, (TOK, TOK), 0)
    tok_at = lax.broadcasted_iota(jnp.int32, (TOK, TOK), 1)
    causal = jnp.concatenate([key_at <= tok_at] * GROUP, axis=1)
    valid = key_at < ln[0]

    def run(*steps):
        most = max(n for _, n in steps)
        done = [0] * len(steps)
        for t in range(1, most + 1):
            for k, (step, n) in enumerate(steps):
                while done[k] * most < t * n and done[k] < n:
                    next(step, None)
                    done[k] += 1
        for step, _ in steps:
            for _ in step:
                pass

    def attend(slabs, at, start, end):
        rows = len(slabs) * TOK
        span = slice(at, at + rows)

        def slab(j):
            if slabs[j] is None:
                return docs[...].reshape(TOK, WIDE)
            return keys[slabs[j][0], slabs[j][1]].reshape(TOK, WIDE)

        for j in range(len(slabs)):
            ct[:, at + j * TOK : at + (j + 1) * TOK] = slab(j)[:, :LAT].T

        def scores(i, k):
            top = None
            step = 5
            for j in range(0, len(slabs), step):
                some = slabs[j : j + step]
                s = dot(jnp.concatenate([slab(j + n) for n in range(len(some))], axis=0), qt[i])
                for n, which in enumerate(some):
                    part = s[n * TOK : (n + 1) * TOK]
                    if which is None:
                        part = jnp.where(causal, part, -1e30)
                    S[k][(j + n) * TOK : (j + n + 1) * TOK] = part
                    m = jnp.max(part.reshape(TOK // 8, 8, N), axis=0)
                    top = m if top is None else jnp.maximum(top, m)
                yield
            new = jnp.broadcast_to(jnp.max(top, axis=0, keepdims=True) * SCALE, (8, N))
            if not start:
                old = mrun[i]
                new = jnp.maximum(old, new)
                al[k] = jnp.exp2(old - new)
            mx[k] = new
            if not end:
                mrun[i] = new
            yield

        def weights(k):
            m = mx[k][:1]
            total = jnp.zeros((8, N), F32)
            for r in range(0, rows, 64):
                w = jnp.exp2(S[k][r : r + 64] * SCALE - m)
                total = total + jnp.sum(w.reshape(8, 8, N), axis=0)
                PR[k][r : r + 64] = w.astype(BF16)
                yield
            sm[k] = total
            yield

        def project(i, k):
            total = sm[k]
            if not start:
                fade = al[k]
                total = total + lrun[i] * fade
            if not end:
                lrun[i] = total
            inverse = 1.0 / jnp.sum(total, axis=0, keepdims=True)
            parts = []
            for r in range(0, LAT, 256):
                o = dot(ct[r : r + 256, span], PR[k][:rows])
                if not start:
                    o = o + acc[i, r : r + 256] * fade[:1]
                if end:
                    parts.append((o * inverse).astype(BF16))
                else:
                    acc[i, r : r + 256] = o
                yield
            if not end:
                return
            o = jnp.concatenate(parts, axis=0)
            for h in range(GROUP):
                cols = pl.ds(pl.multiple_of(i * N + h * DV, DV), DV)
                v = lax.dot_general(
                    o[:, h * TOK : (h + 1) * TOK], uv[:, cols], (((0,), (0,)), ((), ())), preferred_element_type=F32
                )
                out_v[:, cols] = jnp.where(valid, v, 0.0).astype(BF16)
                yield
            cols = pl.ds(pl.multiple_of(i * N, N), N)
            pltpu.make_async_copy(out_v.at[:, cols], out_h.at[:, cols], osem.at[i]).start()
            yield

        def A(i, k):
            return scores(i, k), -(-len(slabs) // 5) + 1

        def B(k):
            return weights(k), rows // 64 + 1

        def C(i, k):
            return project(i, k), 2 + (GROUP + 1 if end else 0)

        return A, B, C

    def loop(stages, extra=None):
        A, B, C = stages

        def body(t, _):
            i = 2 * t + 1
            if extra is not None:
                pl.when(t == 0)(extra)
            run(A(i + 1, 0), B(1), C(i - 1, 0))
            run(A(i + 2, 1), B(0), C(i, 1))
            return 0

        lax.fori_loop(0, GROUPS // 2 - 1, body, 0)

    def join(old, new):
        run(new[0](0, 0), old[1](1), old[2](GROUPS - 2, 0))
        run(new[0](1, 1), new[1](0), old[2](GROUPS - 1, 1))

    for copy in first:
        copy.wait_recv()
    own = send(keys.at[c, b], twin)
    up0, down0 = send(keys.at[c, b], up), send(keys.at[c, b], down)
    prev, nxt, opp, d = (b + 3) % 4, (b + 1) % 4, (b + 2) % 4, 1 - c
    doc_up, doc_down = send(docs.at[ten], t_up), send(docs.at[ten], t_down)
    own.wait_recv()
    crossing = [cross_copy(keys.at[c, b], peer) for peer in (far, far_twin)]

    def cross_over():
        for copy in (up0, down0):
            copy.wait_send()
        sent[:] = [copy for copy in sent if copy is not up0 and copy is not down0]
        for copy in crossing:
            copy.start()

    one = attend([(c, b), (d, a)], 0, True, False)
    run(one[0](0, 0))
    run(one[0](1, 1), one[1](0))
    loop(one, cross_over)
    far0, far1 = crossing
    doc_up.wait_recv()
    doc_far0 = send(docs.at[(ten + 3) % 4, pl.ds(0, 16)], t_up)
    doc_down.wait_recv()
    doc_far1 = send(docs.at[(ten + 1) % 4, pl.ds(16, 16)], t_down)

    up0.wait_recv()
    down0.wait_recv()
    t0, t1 = send(keys.at[c, prev], twin), send(keys.at[c, nxt], twin)
    two = attend([(c, prev), (c, nxt)], 256, False, False)
    join(one, two)
    loop(two)

    for copy in (doc_far0, doc_far1, t0, t1):
        copy.wait_recv()
    three = attend([None, (d, (a + 3) % 4), (d, (a + 1) % 4)], 512, False, False)
    join(two, three)
    loop(three)

    for copy in (far0, far1):
        copy.wait_recv()
    loads["uv"].wait()
    four = attend([(c, opp), (d, (a + 2) % 4)], 896, False, True)
    join(three, four)
    loop(four)
    run(four[2](GROUPS - 2, 0), four[1](1))
    run(four[2](GROUPS - 1, 1))
    for copy in sent:
        copy.wait_send()
    for i in range(GROUPS):
        cols = pl.ds(i * N, N)
        pltpu.make_async_copy(out_v.at[:, cols], out_h.at[:, cols], osem.at[i]).wait()


def per_device(q_nope, q_rope, uk_weight, uv_weight, prompt_latent, prompt_rope, doc_latent, doc_rope, doc_lengths):
    hbm = pl.BlockSpec(memory_space=pl.ANY)
    return pl.pallas_call(
        kernel,
        out_shape=jax.ShapeDtypeStruct((TOK, HEADS * DV), BF16),
        in_specs=[hbm] * 8 + [pl.BlockSpec(memory_space=pltpu.SMEM)],
        out_specs=hbm,
        scratch_shapes=[
            pltpu.VMEM((TOK, HEADS * DN), BF16),
            pltpu.VMEM((TOK, HEADS * DR), BF16),
            pltpu.VMEM((LAT, HEADS * DN), BF16),
            pltpu.VMEM((LAT, HEADS * DV), BF16),
            pltpu.VMEM((16, LAT), BF16),
            pltpu.VMEM((16, DR), BF16),
            pltpu.VMEM((32, LAT), BF16),
            pltpu.VMEM((32, DR), BF16),
            pltpu.VMEM((2, 4, 8, 16, WIDE), BF16),
            pltpu.VMEM((4, 32, WIDE), BF16),
            pltpu.VMEM((LAT, KEYS), BF16),
            pltpu.VMEM((GROUPS, WIDE, N), BF16),
            pltpu.VMEM((384, N), F32),
            pltpu.VMEM((384, N), F32),
            pltpu.VMEM((384, N), BF16),
            pltpu.VMEM((384, N), BF16),
            pltpu.VMEM((2, 8, N), F32),
            pltpu.VMEM((2, 8, N), F32),
            pltpu.VMEM((2, 8, N), F32),
            pltpu.VMEM((GROUPS, LAT, N), F32),
            pltpu.VMEM((GROUPS, 8, N), F32),
            pltpu.VMEM((GROUPS, 8, N), F32),
            pltpu.VMEM((TOK, HEADS * DV), BF16),
            pltpu.SemaphoreType.DMA((11,)),
            pltpu.SemaphoreType.DMA((GROUPS,)),
            pltpu.SemaphoreType.DMA((24,)),
            pltpu.SemaphoreType.DMA((24,)),
        ],
        compiler_params=pltpu.CompilerParams(
            collective_id=0, has_side_effects=True, vmem_limit_bytes=56 * 2**20
        ),
        name="attend",
    )(q_nope, q_rope, uk_weight, uv_weight, prompt_latent, prompt_rope, doc_latent, doc_rope, doc_lengths)


def solution(mesh):
    return jax.shard_map(
        per_device,
        mesh=mesh,
        in_specs=(
            P("dp", "tensor"),
            P("dp", "tensor"),
            P(None, "tensor"),
            P(None, "tensor"),
            P("dp", None),
            P("dp", None),
            P(("dp", "tensor"), None),
            P(("dp", "tensor"), None),
            P("dp"),
        ),
        out_specs=P("dp", "tensor"),
        check_vma=False,
    )
```
